32 devices in a mesh: groups: 2 (over y), replica: 16 (over z, x, core).
Axes of the slice: x: 2, y: 2, z: 4, core: 2. Of those that a mesh axis runs over, the one named last changes fastest.
Arguments:
- first_activations: bfloat16 [4096, 4096], P(('groups', 'replica')), parts along dimension 0, may hold values from -6 to 6
- second_activations: bfloat16 [4096, 4096], P(('groups', 'replica')), parts along dimension 0, may hold values from -6 to 6
- first_adapter_ids: int32 [4096], P(('groups', 'replica')), parts along dimension 0, may hold values from 0 to 63, as said below
- second_adapter_ids: int32 [4096], P(('groups', 'replica')), parts along dimension 0, may hold values from 0 to 63, as said below
- valid_row_counts: int32 [2, 32], P(None, ('groups', 'replica')), parts along dimension 1, may hold values from 64 to 128, as said below
- popular_adapters: int32 [16], P('groups'), parts along dimension 0, may hold values from 0 to 63, as said below
- replica_hosting: int32 [32], P(('groups', 'replica')), parts along dimension 0, may hold values from 0 to 7
- value_weight_base: bfloat16 [4096, 512], replicated, may hold values from -0.09375 to 0.09375
- adapter_down_factors: bfloat16 [64, 4096, 64], P('replica'), may hold values from -0.09375 to 0.09375
- adapter_up_factors: bfloat16 [64, 64, 512], P('replica'), may hold values from -0.75 to 0.75
Outputs:
- first_output: bfloat16 [4096, 512], P(('groups', 'replica')), parts along dimension 0
- second_output: bfloat16 [4096, 512], P(('groups', 'replica')), parts along dimension 0
- resident_down: bfloat16 [32, 4096, 64], P(('groups', 'replica')), parts along dimension 0
- resident_up: bfloat16 [32, 64, 512], P(('groups', 'replica')), parts along dimension 0
The draws below stay inside these ranges and needn't reach their ends.
There are 2 independent parts, one for each index of `groups`. The reference program is written for one: setup_inputs(seed, part) draws one part's arguments, and reference() takes and returns one part's arrays. A program takes and returns all parts, laid end to end along the dimension named above; an argument that names none is the same for every part. Nothing has to cross between parts.
Inputs may be any that keep to these rules, and one draw needn't show every extreme that they name: `first_adapter_ids`: adapter a is homed on replica a // 4. Among the 128 rows of one replica at most 12 name adapters homed on one replica, and in every draw some replica receives exactly 12 from every replica. `second_adapter_ids`: same law as first_adapter_ids, drawn afresh. `valid_row_counts`: in each micro-batch some replica has all 128 rows valid. `popular_adapters`: 8 distinct adapters, homed on distinct replicas.
All inputs are finite; a program needn't handle non-finite values.
Results may differ from the reference program's by a relative error of at most 0.0052.
Values may be sent and summed in bfloat16 or wider, within the bound.
No kernel may reach another device: no remote copies, remote signals or barrier semaphores. Data moves between devices by JAX's collectives and lax.ppermute only.
A program may use at most 64 MiB of HBM per device.

```python
import jax
import jax.numpy as jnp
from jax import lax

MODEL_WIDTH = 4096
VALUE_FEATURES = 512
ADAPTER_RANK = 64
ADP_DEV = 4
HOT = 8
TOK_DEV = 128
ADAPTER_TOTAL = 64
TOKENS = 2048
CAP = 12
N_REPLICA = 16


def hot_layout(key):
    owner_key, slot_key = jax.random.split(key)
    owners = jax.random.permutation(owner_key, N_REPLICA)[:HOT].astype(jnp.int32)
    slots = jax.random.randint(slot_key, (HOT,), 0, ADP_DEV, dtype=jnp.int32)
    return (owners, slots)


def token_adapters(key, salt):
    owners, slots = hot_layout(key)
    key = jax.random.fold_in(key, salt)
    pick_key, shuffle_key, local_key = jax.random.split(key, 3)
    slot_total = N_REPLICA * CAP
    slot_owner = jnp.arange(slot_total, dtype=jnp.int32) // CAP
    hot_flag = jnp.zeros((N_REPLICA,), jnp.int32).at[owners].set(1)
    hot_slot = jnp.zeros((N_REPLICA,), jnp.int32).at[owners].set(slots)
    raw_score = jax.random.randint(pick_key, (N_REPLICA, slot_total), 0, 2 ** 19, dtype=jnp.int32)
    score = (raw_score + hot_flag[slot_owner][None, :] * 2 ** 19) * slot_total + jnp.arange(slot_total, dtype=jnp.int32)[None, :]
    top_values, selected = lax.top_k(score, TOK_DEV)
    chosen_owner = slot_owner[selected]
    mixing = jax.random.randint(shuffle_key, (N_REPLICA, TOK_DEV), 0, 2 ** 19, dtype=jnp.int32) * TOK_DEV + jnp.arange(TOK_DEV, dtype=jnp.int32)[None, :]
    reorder = jnp.argsort(mixing, axis=1, stable=True)
    placed = jnp.take_along_axis(chosen_owner, reorder, axis=1)
    free_slot = jax.random.randint(local_key, (N_REPLICA, TOK_DEV), 0, ADP_DEV, dtype=jnp.int32)
    inside_limit = jnp.where(hot_flag[placed] == 1, hot_slot[placed], free_slot)
    return (placed * ADP_DEV + inside_limit).reshape(N_REPLICA * TOK_DEV)


def draw_first_adapter_ids(key, part):
    return token_adapters(key, 1)


def draw_second_adapter_ids(key, part):
    return token_adapters(key, 2)


def draw_popular_adapters(key, part):
    owners, slots = hot_layout(key)
    return owners * ADP_DEV + slots


def draw_valid_row_counts(key, part):
    key = jax.random.fold_in(key, 5)
    draw_key, pick_key = jax.random.split(key)
    row_limits = jax.random.randint(draw_key, (2, N_REPLICA), TOK_DEV // 2, TOK_DEV + 1, dtype=jnp.int32)
    fullest = jax.random.randint(pick_key, (2,), 0, N_REPLICA, dtype=jnp.int32)
    return row_limits.at[jnp.arange(2, dtype=jnp.int32), fullest].set(TOK_DEV)


def plant(array, rng, low, largest):
    shape = array.shape
    spot = [jax.random.randint(jax.random.fold_in(rng, axis), (), 0, shape[axis]) for axis in range(len(shape))]
    array = array.at[tuple(spot)].set(low)
    longest = shape.index(max(shape))
    spot[longest] = (spot[longest] + 1) % shape[longest]
    return array.at[tuple(spot)].set(largest)


def levels(stream_key, dims, cuts, least, top_value):
    factor_of = 1.0
    for dim, parts in cuts:
        steps = jax.random.uniform(jax.random.fold_in(jax.random.fold_in(stream_key, 6), dim), (parts,), jnp.float32, least / len(cuts), top_value / len(cuts))
        factor_of = factor_of * jnp.repeat(jnp.exp(steps), dims[dim] // parts).reshape((-1,) + (1,) * (len(dims) - 1 - dim))
    return factor_of


def scatter_about(own_key, dims, deviation, reach, cuts=(), held_as=jnp.bfloat16):
    values = deviation * jax.random.normal(own_key, dims, jnp.float32)
    if cuts:
        values = values * levels(own_key, dims, cuts, -0.22, 0.18)
    return jnp.clip(values, -reach, reach).astype(held_as)


def setup_inputs(seed: int = 0, part: int = 0) -> dict:
    arg_keys = jax.random.split(jax.random.key(seed), 11)
    own_keys = jax.random.split(jax.random.fold_in(arg_keys[10], part), 11)
    first_activations = scatter_about(own_keys[0], (TOKENS, MODEL_WIDTH), 1.0, 6.0, ((0, 16),))
    second_activations = scatter_about(own_keys[1], (TOKENS, MODEL_WIDTH), 1.0, 6.0, ((0, 16),))
    first_adapter_ids = draw_first_adapter_ids(jax.random.fold_in(jax.random.fold_in(arg_keys[10], part), 71), part)
    second_adapter_ids = draw_second_adapter_ids(jax.random.fold_in(jax.random.fold_in(arg_keys[10], part), 71), part)
    valid_row_counts = draw_valid_row_counts(jax.random.fold_in(jax.random.fold_in(arg_keys[10], part), 71), part)
    popular_adapters = draw_popular_adapters(jax.random.fold_in(jax.random.fold_in(arg_keys[10], part), 71), part)
    replica_hosting = plant(jax.random.randint(own_keys[6], (N_REPLICA,), 0, HOT), jax.random.fold_in(own_keys[6], 1), 0, HOT - 1).astype(jnp.int32)
    value_weight_base = scatter_about(arg_keys[7], (MODEL_WIDTH, VALUE_FEATURES), MODEL_WIDTH ** -0.5, 0.09375)
    adapter_down_factors = scatter_about(arg_keys[8], (ADAPTER_TOTAL, MODEL_WIDTH, ADAPTER_RANK), MODEL_WIDTH ** -0.5, 0.09375, ((0, 16),))
    adapter_up_factors = scatter_about(arg_keys[9], (ADAPTER_TOTAL, ADAPTER_RANK, VALUE_FEATURES), ADAPTER_RANK ** -0.5, 0.75, ((0, 16),))
    return dict(first_activations=first_activations, second_activations=second_activations, first_adapter_ids=first_adapter_ids, second_adapter_ids=second_adapter_ids, valid_row_counts=valid_row_counts, popular_adapters=popular_adapters, replica_hosting=replica_hosting, value_weight_base=value_weight_base, adapter_down_factors=adapter_down_factors, adapter_up_factors=adapter_up_factors)


def adapter_update(token_rows, selected, adapter_down_factors, adapter_up_factors):
    block = 64 if TOKENS % 64 == 0 else TOK_DEV
    count = TOKENS // block
    row_blocks = token_rows.reshape(count, block, MODEL_WIDTH)
    chosen_blocks = selected.reshape(count, block)

    def one_block(pair):
        block_rows, block_numbers = pair
        down_factor_rows = adapter_down_factors[block_numbers].astype(jnp.float32)
        projected = jnp.einsum("td,tdr->tr", block_rows.astype(jnp.float32), down_factor_rows).astype(jnp.bfloat16)
        up_factor_rows = adapter_up_factors[block_numbers].astype(jnp.float32)
        return jnp.einsum("tr,trk->tk", projected.astype(jnp.float32), up_factor_rows).astype(jnp.bfloat16)

    return lax.map(one_block, (row_blocks, chosen_blocks)).reshape(TOKENS, VALUE_FEATURES)


def single_batch(token_rows, selected, row_limits, value_weight_base, adapter_down_factors, adapter_up_factors):
    positions = jnp.arange(TOKENS, dtype=jnp.int32)
    valid = (positions % TOK_DEV) < row_limits[positions // TOK_DEV]
    lowrank_update = adapter_update(token_rows, selected, adapter_down_factors, adapter_up_factors)
    base = jnp.dot(token_rows, value_weight_base, preferred_element_type=jnp.float32)
    summed = (base + lowrank_update.astype(jnp.float32)).astype(jnp.bfloat16)
    return jnp.where(valid[:, None], summed, jnp.zeros((), jnp.bfloat16))


def reference(first_activations, second_activations, first_adapter_ids, second_adapter_ids, valid_row_counts, popular_adapters, replica_hosting, value_weight_base, adapter_down_factors, adapter_up_factors):
    first_output = single_batch(first_activations, first_adapter_ids, valid_row_counts[0], value_weight_base, adapter_down_factors, adapter_up_factors)
    second_output = single_batch(second_activations, second_adapter_ids, valid_row_counts[1], value_weight_base, adapter_down_factors, adapter_up_factors)
    hosted_adapters = popular_adapters[replica_hosting]
    return first_output, second_output, adapter_down_factors[hosted_adapters], adapter_up_factors[hosted_adapters]
```

```python
import functools
import math

import jax
import jax.numpy as jnp
from jax import lax
from jax.experimental import pallas as pl
from jax.experimental.pallas import tpu as pltpu
from jax.sharding import PartitionSpec as P

LANES = 128
ROWS = 16
CHUNK = 256
F32 = jnp.float32
BF16 = jnp.bfloat16


class Plan:
    def __init__(self, peers, tok, width, rank, feature, homed):
        self.peers, self.tok, self.width, self.rank = peers, tok, width, rank
        self.feature, self.homed = feature, homed
        self.cap = max(2, 3 * tok // (2 * peers))
        g = math.gcd(self.cap, ROWS)
        self.keep = self.cap // g
        self.pieces = ROWS // g
        self.extra = self.pieces - self.keep
        self.piece = width // self.pieces
        self.back = 2 * feature // self.pieces
        self.packed = peers * ROWS
        self.chunk = min(CHUNK, self.packed)
        self.row_groups = rank // ROWS
        self.col_tiles = (width + feature) // LANES
        self.tiles = self.row_groups * self.col_tiles
        self.share = -(-self.tiles // peers)
        self.tok_cols = self.keep * self.piece
        self.spread_cols = self.share * LANES
        self.back_cols = self.keep * self.back
        self.out_cols = 2 * self.tok_cols + self.spread_cols + LANES
        self.ret_cols = self.spread_cols + self.back_cols

    def chunks(self, body):
        count = self.packed // self.chunk
        if count == 1:
            body(0)
        else:

            @pl.loop(0, count)
            def _(i):
                body(pl.multiple_of(i * self.chunk, self.chunk))

    def extra_place(self, position, q):
        index = position * self.extra + (q - self.keep)
        row = index // self.keep
        return self.cap + row, index - row * self.keep


def route(ids_row, homed):
    n = ids_row.shape[1]
    ids = jnp.broadcast_to(ids_row, (n, n))
    peer_row = ids // homed
    peer_col = jnp.transpose(ids.astype(F32)).astype(jnp.int32) // homed
    same = peer_row == peer_col
    above = lax.broadcasted_iota(jnp.int32, (n, n), 0)
    along = lax.broadcasted_iota(jnp.int32, (n, n), 1)
    pos_row = jnp.sum(jnp.where(same & (above < along), 1, 0), axis=0, keepdims=True)
    pos_col = jnp.sum(jnp.where(same & (along < above), 1, 0), axis=1, keepdims=True)
    return peer_row[0:1, :], pos_row, peer_col[:, 0:1], pos_col


def pack_kernel(plan, ids1, ids2, popular, hosting, x1, x2, down, up, out):
    me = lax.axis_index("replica")
    slot = jnp.int32(0)
    for i in range(popular.shape[0]):
        adapter = popular[i]
        slot = jnp.where(adapter // plan.homed == me, adapter % plan.homed, slot)
    wanted = popular[hosting[0]] // plan.homed
    base = 2 * plan.tok_cols
    for t in range(plan.share * plan.peers):
        d, j = divmod(t, plan.share)
        to = (pl.ds(d * ROWS, ROWS), pl.ds(base + j * LANES, LANES))
        if t < plan.tiles:
            group, col = divmod(t, plan.col_tiles)
            rows = pl.ds(group * ROWS, ROWS)
            col *= LANES
            if col < plan.width:
                out[to] = down[slot, rows, pl.ds(col, LANES)]
            else:
                out[to] = up[slot, rows, pl.ds(col - plan.width, LANES)]
        else:
            out[to] = jnp.zeros((ROWS, LANES), BF16)
    routes = []
    for ids in (ids1, ids2):
        peer, pos, _, _ = route(ids[...], plan.homed)
        routes.append((peer, pos, (ids[...] % plan.homed).astype(F32)))

    def body(start):
        index = lax.broadcasted_iota(jnp.int32, (plan.chunk, plan.tok), 0) + start
        meta = jnp.zeros((plan.chunk, LANES), F32)
        lane = lax.broadcasted_iota(jnp.int32, (plan.chunk, LANES), 1)
        rows = pl.ds(start, plan.chunk)
        for b, x in enumerate((x1, x2)):
            peer, pos, slots = routes[b]
            direct = index == peer * ROWS + pos
            slot_col = jnp.sum(jnp.where(direct, slots, 0.0), axis=1, keepdims=True)
            meta = jnp.where(lane == b, slot_col, meta)
            ends = [plan.extra_place(pos, q) for q in range(plan.keep, plan.pieces)]
            for k in range(plan.keep):
                hots = [direct] + [(index == peer * ROWS + r) & (blk == k) for r, blk in ends]
                parts = [x[:, k * plan.piece : (k + 1) * plan.piece]]
                parts += [
                    x[:, q * plan.piece : (q + 1) * plan.piece]
                    for q in range(plan.keep, plan.pieces)
                ]
                hot = jnp.concatenate(
                    [jnp.where(h, 1.0, 0.0).astype(BF16) for h in hots], axis=1
                )
                got = jnp.dot(hot, jnp.concatenate(parts, axis=0), preferred_element_type=F32)
                col = b * plan.tok_cols + k * plan.piece
                out[rows, col : col + plan.piece] = got.astype(BF16)
        meta = jnp.where(lane == 2, wanted.astype(F32), meta)
        out[rows, base + plan.spread_cols :] = meta.astype(BF16)

    plan.chunks(body)


def home_kernel(plan, got, down, up, out):
    base = 2 * plan.tok_cols
    joined = plan.homed * plan.rank

    def unpack(start, first, size, q, into):
        n = plan.chunk
        row = lax.broadcasted_iota(jnp.int32, (n, n), 0)
        col = lax.broadcasted_iota(jnp.int32, (n, n), 1)
        p = row % ROWS
        place, blk = plan.extra_place(p, q)
        target = row - p + place
        rows = pl.ds(start, n)
        total = None
        hots = [
            jnp.where((col == target) & (blk == k) & (p < plan.cap), 1.0, 0.0).astype(BF16)
            for k in range(plan.keep)
        ]
        parts = [got[rows, first + k * size : first + (k + 1) * size] for k in range(plan.keep)]
        return jnp.dot(
            jnp.concatenate(hots, axis=1),
            jnp.concatenate(parts, axis=0),
            preferred_element_type=F32,
        ).astype(BF16)

    def body(start):
        n = plan.chunk
        rows = pl.ds(start, n)
        meta = got[rows, base + plan.spread_cols : base + plan.spread_cols + LANES].astype(F32)
        meta = meta.astype(jnp.int32)
        deltas = []
        nt = (((1,), (1,)), ((), ()))
        for b in range(2):
            first = b * plan.tok_cols
            total = lax.dot_general(
                got[rows, first : first + plan.tok_cols],
                down[:, : plan.tok_cols],
                nt,
                preferred_element_type=F32,
            )
            for q in range(plan.keep, plan.pieces):
                total += lax.dot_general(
                    unpack(start, first, plan.piece, q, None),
                    down[:, q * plan.piece : (q + 1) * plan.piece],
                    nt,
                    preferred_element_type=F32,
                )
            column = lax.broadcasted_iota(jnp.int32, (n, joined), 1) // plan.rank
            kept = jnp.where(column == meta[:, b : b + 1], total, 0.0).astype(BF16)
            deltas.append(
                jnp.dot(kept, up[...], preferred_element_type=F32).astype(BF16)
            )
        both = jnp.concatenate(deltas, axis=1)
        row = lax.broadcasted_iota(jnp.int32, (n, n), 0)
        col = lax.broadcasted_iota(jnp.int32, (n, n), 1)
        p = col % ROWS
        straight = (row == col) & (p < plan.cap)
        ends = [plan.extra_place(p, q) for q in range(plan.keep, plan.pieces)]
        for k in range(plan.keep):
            hots = [straight] + [
                (row == col - p + r) & (blk == k) & (p < plan.cap) for r, blk in ends
            ]
            parts = [both[:, k * plan.back : (k + 1) * plan.back]] + [
                both[:, q * plan.back : (q + 1) * plan.back]
                for q in range(plan.keep, plan.pieces)
            ]
            hot = jnp.concatenate([jnp.where(h, 1.0, 0.0).astype(BF16) for h in hots], axis=1)
            sent = jnp.dot(hot, jnp.concatenate(parts, axis=0), preferred_element_type=F32)
            at = plan.spread_cols + k * plan.back
            out[rows, at : at + plan.back] = sent.astype(BF16)
        wide = lax.broadcasted_iota(jnp.int32, (n, plan.packed), 1)
        inner = lax.broadcasted_iota(jnp.int32, (n, plan.packed), 0) % ROWS
        pick = jnp.where(wide == meta[:, 2:3] * ROWS + inner, 1.0, 0.0).astype(BF16)
        out[rows, : plan.spread_cols] = jnp.dot(
            pick, got[:, base : base + plan.spread_cols], preferred_element_type=F32
        ).astype(BF16)

    plan.chunks(body)


def final_kernel(plan, ids1, ids2, counts, back, base1, base2, out1, out2, down, up):
    for t in range(plan.tiles):
        d, j = divmod(t, plan.share)
        group, col = divmod(t, plan.col_tiles)
        tile = back[d * ROWS : (d + 1) * ROWS, j * LANES : (j + 1) * LANES]
        rows = slice(group * ROWS, (group + 1) * ROWS)
        col *= LANES
        if col < plan.width:
            down[0, rows, col : col + LANES] = tile
        else:
            up[0, rows, col - plan.width : col - plan.width + LANES] = tile
    index = lax.broadcasted_iota(jnp.int32, (plan.tok, plan.packed), 1)
    half = plan.pieces // 2
    for b, (ids, base, out) in enumerate(((ids1, base1, out1), (ids2, base2, out2))):
        _, _, peer, pos = route(ids[...], plan.homed)
        valid = lax.broadcasted_iota(jnp.int32, (plan.tok, plan.back), 0) < counts[b, 0]
        for i in range(half):
            q = b * half + i
            if q < plan.keep:
                hots = [index == peer * ROWS + pos]
                blocks = [q]
            else:
                r, blk = plan.extra_place(pos, q)
                hots = [(index == peer * ROWS + r) & (blk == k) for k in range(plan.keep)]
                blocks = range(plan.keep)
            delta = None
            for h, k in zip(hots, blocks):
                at = plan.spread_cols + k * plan.back
                term = jnp.dot(
                    jnp.where(h, 1.0, 0.0).astype(BF16),
                    back[:, at : at + plan.back],
                    preferred_element_type=F32,
                )
                delta = term if delta is None else delta + term
            cols = slice(i * plan.back, (i + 1) * plan.back)
            out[:, cols] = jnp.where(valid, base[:, cols] + delta, 0.0).astype(BF16)


def local(
    first_activations,
    second_activations,
    first_adapter_ids,
    second_adapter_ids,
    valid_row_counts,
    popular_adapters,
    replica_hosting,
    value_weight_base,
    adapter_down_factors,
    adapter_up_factors,
):
    tok, width = first_activations.shape
    homed, _, rank = adapter_down_factors.shape
    feature = adapter_up_factors.shape[2]
    plan = Plan(lax.axis_size("replica"), tok, width, rank, feature, homed)
    down = jnp.swapaxes(adapter_down_factors, 1, 2)
    ids1 = first_adapter_ids.reshape(1, tok)
    ids2 = second_adapter_ids.reshape(1, tok)
    vmem = pl.BlockSpec(memory_space=pltpu.VMEM)
    smem = pl.BlockSpec(memory_space=pltpu.SMEM)
    params = pltpu.CompilerParams(vmem_limit_bytes=48 * 1024 * 1024)

    sent = pl.pallas_call(
        functools.partial(pack_kernel, plan),
        out_shape=jax.ShapeDtypeStruct((plan.packed, plan.out_cols), BF16),
        in_specs=[vmem, vmem, smem, smem, vmem, vmem, vmem, vmem],
        out_specs=vmem,
        compiler_params=params,
        name="pack",
    )(
        ids1,
        ids2,
        popular_adapters,
        replica_hosting,
        first_activations,
        second_activations,
        down,
        adapter_up_factors,
    )
    exchange = functools.partial(
        lax.all_to_all, axis_name="replica", split_axis=0, concat_axis=0, tiled=True
    )
    got = exchange(sent.reshape(plan.peers, ROWS, plan.out_cols))
    base1 = jnp.dot(first_activations, value_weight_base, preferred_element_type=F32)
    base2 = jnp.dot(second_activations, value_weight_base, preferred_element_type=F32)
    reply = pl.pallas_call(
        functools.partial(home_kernel, plan),
        out_shape=jax.ShapeDtypeStruct((plan.packed, plan.ret_cols), BF16),
        in_specs=[vmem, vmem, vmem],
        out_specs=vmem,
        compiler_params=params,
        name="home",
    )(
        got.reshape(plan.packed, plan.out_cols),
        down.reshape(homed * rank, width),
        adapter_up_factors.reshape(homed * rank, feature),
    )
    back = exchange(reply.reshape(plan.peers, ROWS, plan.ret_cols))
    out1, out2, resident_down, resident_up = pl.pallas_call(
        functools.partial(final_kernel, plan),
        out_shape=[
            jax.ShapeDtypeStruct((tok, feature), BF16),
            jax.ShapeDtypeStruct((tok, feature), BF16),
            jax.ShapeDtypeStruct((1, rank, width), BF16),
            jax.ShapeDtypeStruct((1, rank, feature), BF16),
        ],
        in_specs=[vmem, vmem, smem, vmem, vmem, vmem],
        out_specs=[vmem] * 4,
        compiler_params=params,
        name="finish",
    )(
        ids1,
        ids2,
        valid_row_counts,
        back.reshape(plan.packed, plan.ret_cols),
        base1,
        base2,
    )
    return out1, out2, jnp.swapaxes(resident_down, 1, 2), resident_up


def solution(mesh):
    return jax.shard_map(
        local,
        mesh=mesh,
        in_specs=(
            P(("groups", "replica"), None),
            P(("groups", "replica"), None),
            P(("groups", "replica")),
            P(("groups", "replica")),
            P(None, ("groups", "replica")),
            P("groups"),
            P(("groups", "replica")),
            P(),
            P("replica", None, None),
            P("replica", None, None),
        ),
        out_specs=(
            P(("groups", "replica"), None),
            P(("groups", "replica"), None),
            P(("groups", "replica"), None, None),
            P(("groups", "replica"), None, None),
        ),
        check_vma=False,
    )
```

```python
import functools

import jax
import jax.numpy as jnp
from jax import lax
from jax.experimental import pallas as pl
from jax.experimental.pallas import tpu as pltpu
from jax.sharding import PartitionSpec as P

LANES = 128
ROWS = 16
CHUNK = 256
F32 = jnp.float32
BF16 = jnp.bfloat16
NT = (((1,), (1,)), ((), ()))


class Plan:
    def __init__(self, peers, tok, width, rank, feature, homed):
        self.peers, self.tok, self.width, self.rank = peers, tok, width, rank
        self.feature, self.homed = feature, homed
        self.cap = max(2, 3 * tok // (2 * peers))
        combined = 2 * self.cap
        self.full = combined // ROWS
        left = combined - self.full * ROWS
        if left > 8:
            self.full, left = self.full + 1, 0
        self.rest = left > 0
        self.sections = self.full + self.rest
        self.packed = peers * ROWS
        self.joined = homed * rank
        self.tok_cols = self.full * width + self.rest * (width // 2)
        self.back_cols = self.full * feature + self.rest * (feature // 2)
        self.col_tiles = (width + feature) // LANES
        tiles = (rank // ROWS) * self.col_tiles
        share = -(-tiles // peers)
        while self.col_tiles % share:
            share += 1
        self.per_group = self.col_tiles // share
        self.holders = tiles // share
        self.spread = share * LANES
        self.meta_at = self.tok_cols + self.spread
        self.cols = self.meta_at + LANES
        self.ret_cols = self.spread + self.back_cols
        self.half = peers // 2
        self.split = False and peers & (peers - 1) == 0 and self.half % self.per_group == 0

    def pieces(self, part, me):
        if part == "all":
            return 0, [(0, self.peers)]
        mine = (me // self.half) * self.half
        if part == "near":
            return mine, [(mine, self.half)]
        far = self.half - mine
        partner = me - mine
        return far, [(far + xor(partner, m, self.half), 1) for m in range(self.half)]

    def row_chunks(self, count):
        size = min(CHUNK, count * ROWS)
        return [(i, size) for i in range(0, count * ROWS, size)]


def xor(a, b, bound):
    out, bit = 0, 1
    while bit < bound:
        digit = (a // bit) % 2
        out = out + (1 - digit if b & bit else digit) * bit
        bit *= 2
    return out


def route(ids, homed):
    n = ids.shape[1]
    ids = jnp.broadcast_to(ids, (n, n))
    peer_row = ids // homed
    peer_col = jnp.transpose(ids.astype(F32)).astype(jnp.int32) // homed
    same = peer_row == peer_col
    above = lax.broadcasted_iota(jnp.int32, (n, n), 0)
    along = lax.broadcasted_iota(jnp.int32, (n, n), 1)
    pos_row = jnp.sum(jnp.where(same & (above < along), 1, 0), axis=0, keepdims=True)
    pos_col = jnp.sum(jnp.where(same & (along < above), 1, 0), axis=1, keepdims=True)
    return peer_row[0:1, :], pos_row, peer_col[:, 0:1], pos_col


def as_hot(mask):
    return jnp.where(mask, 1.0, 0.0).astype(BF16)


def pack_kernel(plan, part, ids1, ids2, popular, hosting, x1, x2, down, up, *refs):
    me = lax.axis_index("replica")
    first, arrays = plan.pieces(part, me)
    if part == "near":
        refs = refs[1:]
    outs, (ids, hot_ids, host_id, x, hot, packed, sems, out_sems) = (
        refs[: len(arrays)],
        refs[len(arrays) :],
    )
    count = sum(c for _, c in arrays)
    quarter = plan.width // 4
    loads = [
        pltpu.make_async_copy(popular, hot_ids, sems.at[0]),
        pltpu.make_async_copy(hosting, host_id, sems.at[1]),
        pltpu.make_async_copy(ids1, ids.at[0], sems.at[2]),
        pltpu.make_async_copy(ids2, ids.at[1], sems.at[3]),
    ]
    for c in range(4):
        cols = pl.ds(c * quarter, quarter)
        for b, src in enumerate((x1, x2)):
            loads.append(
                pltpu.make_async_copy(
                    src.at[:, cols],
                    x.at[pl.ds(b * plan.tok, plan.tok), cols],
                    sems.at[4 + 2 * c + b],
                )
            )
    for load in loads:
        load.start()
    loads[0].wait()
    loads[1].wait()
    slot = jnp.int32(0)
    for i in range(hot_ids.shape[0]):
        adapter = hot_ids[i]
        slot = jnp.where(adapter // plan.homed == me, adapter % plan.homed, slot)
    wanted = hot_ids[host_id[0]] // plan.homed
    hots = [
        pltpu.make_async_copy(down.at[slot], hot.at[:, pl.ds(0, plan.width)], sems.at[12]),
        pltpu.make_async_copy(up.at[slot], hot.at[:, pl.ds(plan.width, plan.feature)], sems.at[13]),
    ]
    for load in hots:
        load.start()
    loads[2].wait()
    loads[3].wait()
    peers, cells, slots = [], [], []
    for b in range(2):
        peer, pos, _, _ = route(ids[b], plan.homed)
        peers.append(peer - first)
        cells.append(pos + b * plan.cap)
        slots.append((ids[b] % plan.homed).astype(F32))
    peer, cell = jnp.concatenate(peers, axis=1), jnp.concatenate(cells, axis=1)
    slots = jnp.concatenate(slots, axis=1)
    chunks = plan.row_chunks(count)
    stores = []

    def send(at, size):
        for out, (peer0, n) in zip(outs, arrays):
            stores.append(
                pltpu.make_async_copy(
                    packed.at[pl.ds(pl.multiple_of((peer0 - first) * ROWS, ROWS), n * ROWS),
                              pl.ds(at, size)],
                    out.at[:, pl.ds(at, size)],
                    out_sems.at[len(stores)],
                )
            )
            stores[-1].start()

    masks = []
    for start, size in chunks:
        index = lax.broadcasted_iota(jnp.int32, (size, 2 * plan.tok), 0) + start
        own = index // ROWS == peer
        inner = index % ROWS
        sets = [own & (inner + s * ROWS == cell) for s in range(plan.full)]
        marks = list(sets)
        if plan.rest:
            low = own & (inner + plan.full * ROWS == cell) & (inner < 8)
            high = own & (inner - 8 + plan.full * ROWS == cell) & (inner >= 8)
            sets += [low, high]
            marks.append(low | high)
        masks.append([as_hot(m) for m in sets])
        lane = lax.broadcasted_iota(jnp.int32, (size, LANES), 1)
        meta = jnp.where(lane == plan.sections, wanted.astype(F32), 0.0)
        for s, mark in enumerate(marks):
            value = jnp.sum(jnp.where(mark, slots, 0.0), axis=1, keepdims=True)
            meta = jnp.where(lane == s, value, meta)
        packed[start : start + size, plan.meta_at :] = meta.astype(BF16)

    for c in range(4):
        loads[4 + 2 * c].wait()
        loads[5 + 2 * c].wait()
        cols = slice(c * quarter, (c + 1) * quarter)
        for (start, size), hot_masks in zip(chunks, masks):
            for s in range(plan.full):
                value = jnp.dot(hot_masks[s], x[:, cols], preferred_element_type=F32)
                at = s * plan.width + c * quarter
                packed[start : start + size, at : at + quarter] = value.astype(BF16)
        for s in range(plan.full):
            send(s * plan.width + c * quarter, quarter)
    if plan.rest:
        at = plan.full * plan.width
        for c in range(2):
            for (start, size), hot_masks in zip(chunks, masks):
                both = jnp.concatenate(hot_masks[plan.full :], axis=1)
                source = jnp.concatenate(
                    [
                        x[:, c * quarter : (c + 1) * quarter],
                        x[:, (c + 2) * quarter : (c + 3) * quarter],
                    ],
                    axis=0,
                )
                value = jnp.dot(both, source, preferred_element_type=F32)
                packed[start : start + size, at + c * quarter : at + (c + 1) * quarter] = (
                    value.astype(BF16)
                )
            send(at + c * quarter, quarter)
    for load in hots:
        load.wait()
    for i in range(count):
        peer0, group0 = (i % plan.holders, 0) if part == "all" else (i, first // plan.per_group)
        group = group0 + peer0 // plan.per_group
        col = (peer0 % plan.per_group) * plan.spread
        packed[i * ROWS : (i + 1) * ROWS, plan.tok_cols : plan.meta_at] = hot[
            pl.ds(pl.multiple_of(group * ROWS, ROWS), ROWS), col : col + plan.spread
        ]
    send(plan.tok_cols, plan.spread + LANES)
    for store in stores:
        store.wait()


def home_kernel(plan, parts, down, up, *refs):
    me = lax.axis_index("replica")
    arrays = [a for part in parts for a in plan.pieces(part, me)[1]]
    gots, out, (got, reply, sems, out_sems) = (
        refs[: len(arrays)],
        refs[len(arrays)],
        refs[len(arrays) + 1 :],
    )
    bounds = [(plan.tok_cols, plan.spread + LANES)]
    bounds += [(c, plan.width // 2) for c in range(0, plan.tok_cols, plan.width // 2)]
    loads = []
    for at, size in bounds:
        group = []
        for ref, (peer0, n) in zip(gots, arrays):
            group.append(
                pltpu.make_async_copy(
                    ref.at[:, pl.ds(at, size)],
                    got.at[pl.ds(pl.multiple_of(peer0 * ROWS, ROWS), n * ROWS), pl.ds(at, size)],
                    sems.at[len(loads) * len(arrays) + len(group)],
                )
            )
            group[-1].start()
        loads.append(group)

    def ready(i):
        for load in loads[i]:
            load.wait()

    chunks = plan.row_chunks(plan.peers)
    ready(0)
    metas = []
    for start, n in chunks:
        rows = slice(start, start + n)
        meta = got[rows, plan.meta_at :].astype(F32).astype(jnp.int32)
        metas.append(meta)
        wide = lax.broadcasted_iota(jnp.int32, (n, plan.packed), 1)
        inner = lax.broadcasted_iota(jnp.int32, (n, plan.packed), 0) % ROWS
        pick = as_hot(wide == meta[:, plan.sections : plan.sections + 1] * ROWS + inner)
        reply[rows, : plan.spread] = jnp.dot(
            pick, got[:, plan.tok_cols : plan.meta_at], preferred_element_type=F32
        ).astype(BF16)
    relayed = pltpu.make_async_copy(
        reply.at[:, pl.ds(0, plan.spread)], out.at[:, pl.ds(0, plan.spread)], out_sems.at[0]
    )
    relayed.start()
    half = plan.width // 2
    group = plan.joined
    for s in range(plan.sections):
        at = s * plan.width
        split = s == plan.full
        ready(1 + 2 * s)
        for i, ((start, n), meta) in enumerate(zip(chunks, metas)):
            rows = slice(start, start + n)
            low = lax.dot_general(
                got[rows, at : at + half], down[:, :half], NT, preferred_element_type=F32
            )
            if not split:
                if i == 0:
                    ready(2 + 2 * s)
                low += lax.dot_general(
                    got[rows, at + half : at + plan.width],
                    down[:, half:],
                    NT,
                    preferred_element_type=F32,
                )
                slot = meta[:, s : s + 1]
            else:
                high = lax.dot_general(
                    got[rows, at : at + half], down[:, half:], NT, preferred_element_type=F32
                )
                low = low.reshape(n // ROWS, 2, 8, group)[:, 0]
                high = high.reshape(n // ROWS, 2, 8, group)[:, 1]
                low = (low + high).reshape(n // 2, group)
                slot = meta.reshape(n // ROWS, 2, 8, LANES)[:, 0].reshape(n // 2, LANES)
                slot = slot[:, s : s + 1]
            column = lax.broadcasted_iota(jnp.int32, low.shape, 1) // plan.rank
            kept = jnp.where(column == slot, low, 0.0).astype(BF16)
            delta = jnp.dot(kept, up[...], preferred_element_type=F32)
            to = plan.spread + s * plan.feature
            if split:
                delta = delta.reshape(n // ROWS, 8, plan.feature)
                middle = plan.feature // 2
                delta = jnp.concatenate([delta[..., :middle], delta[..., middle:]], axis=1)
                delta = delta.reshape(n, middle)
            reply[rows, to : to + delta.shape[1]] = delta.astype(BF16)
    answered = pltpu.make_async_copy(
        reply.at[:, pl.ds(plan.spread, plan.back_cols)],
        out.at[:, pl.ds(plan.spread, plan.back_cols)],
        out_sems.at[1],
    )
    answered.start()
    relayed.wait()
    answered.wait()


def final_kernel(plan, ids1, ids2, counts, back, base1, base2, out1, out2, down, up):
    for d in range(plan.holders):
        rows = slice((d // plan.per_group) * ROWS, (d // plan.per_group + 1) * ROWS)
        for j in range(0, plan.spread, LANES):
            col = (d % plan.per_group) * plan.spread + j
            tile = back[d * ROWS : (d + 1) * ROWS, j : j + LANES]
            if col < plan.width:
                down[0, rows, col : col + LANES] = tile
            else:
                up[0, rows, col - plan.width : col - plan.width + LANES] = tile
    index = lax.broadcasted_iota(jnp.int32, (plan.tok, plan.packed), 1)
    inner = index % ROWS
    middle = plan.feature // 2
    for b, (ids, base, out) in enumerate(((ids1, base1, out1), (ids2, base2, out2))):
        _, _, peer, pos = route(ids[...], plan.homed)
        cell = pos + b * plan.cap
        own = index // ROWS == peer
        total = base[...]
        for s in range(plan.full):
            if (b + 1) * plan.cap <= s * ROWS or b * plan.cap >= (s + 1) * ROWS:
                continue
            hot = as_hot(own & (inner + s * ROWS == cell))
            at = plan.spread + s * plan.feature
            total += jnp.dot(hot, back[:, at : at + plan.feature], preferred_element_type=F32)
        if plan.rest and (b + 1) * plan.cap > plan.full * ROWS:
            at = plan.spread + plan.full * plan.feature
            values = back[:, at : at + middle]
            low = as_hot(own & (inner + plan.full * ROWS == cell) & (inner < 8))
            high = as_hot(own & (inner - 8 + plan.full * ROWS == cell) & (inner >= 8))
            total += jnp.concatenate(
                [jnp.dot(hot, values, preferred_element_type=F32) for hot in (low, high)], axis=1
            )
        valid = lax.broadcasted_iota(jnp.int32, total.shape, 0) < counts[b, 0]
        out[...] = jnp.where(valid, total, 0.0).astype(BF16)


def local(
    first_activations,
    second_activations,
    first_adapter_ids,
    second_adapter_ids,
    valid_row_counts,
    popular_adapters,
    replica_hosting,
    value_weight_base,
    adapter_down_factors,
    adapter_up_factors,
):
    tok, width = first_activations.shape
    homed, _, rank = adapter_down_factors.shape
    feature = adapter_up_factors.shape[2]
    plan = Plan(lax.axis_size("replica"), tok, width, rank, feature, homed)
    peers, half = plan.peers, plan.half
    down = jnp.swapaxes(adapter_down_factors, 1, 2)
    ids1 = first_adapter_ids.reshape(1, tok)
    ids2 = second_adapter_ids.reshape(1, tok)
    anywhere = pl.BlockSpec(memory_space=pl.ANY)
    vmem = pl.BlockSpec(memory_space=pltpu.VMEM)
    smem = pl.BlockSpec(memory_space=pltpu.SMEM)
    params = pltpu.CompilerParams(vmem_limit_bytes=60 * 1024 * 1024)

    def pack(part, *after):
        sizes = {"all": [peers], "near": [half], "far": [1] * half}[part]
        return pl.pallas_call(
            functools.partial(pack_kernel, plan, part),
            out_shape=[jax.ShapeDtypeStruct((n * ROWS, plan.cols), BF16) for n in sizes],
            in_specs=[anywhere] * (8 + len(after)),
            out_specs=[anywhere] * len(sizes),
            scratch_shapes=[
                pltpu.VMEM((2, 1, tok), jnp.int32),
                pltpu.SMEM(popular_adapters.shape, jnp.int32),
                pltpu.SMEM(replica_hosting.shape, jnp.int32),
                pltpu.VMEM((2 * tok, width), BF16),
                pltpu.VMEM((rank, width + feature), BF16),
                pltpu.VMEM((sum(sizes) * ROWS, plan.cols), BF16),
                pltpu.SemaphoreType.DMA((14,)),
                pltpu.SemaphoreType.DMA((len(sizes) * (4 * plan.full + 2 * plan.rest + 1),)),
            ],
            compiler_params=params,
            name="pack_" + part,
        )(
            ids1,
            ids2,
            popular_adapters,
            replica_hosting,
            first_activations,
            second_activations,
            down,
            adapter_up_factors,
            *after,
        )

    def exchange(x, n, **kwargs):
        x = x.reshape(n, x.shape[0] // n, x.shape[1])
        x = lax.all_to_all(x, "replica", split_axis=0, concat_axis=0, tiled=True, **kwargs)
        return x.reshape(n * x.shape[1], x.shape[2])

    if plan.split:
        parts = ("far", "near")
        gots = []
        far = pack("far")
        for m, block in enumerate(far):
            pairs = [(i, i ^ (m + half)) for i in range(peers)]
            gots.append(lax.ppermute(block, "replica", pairs))
        halves = [list(range(half)), list(range(half, peers))]
        near, _ = lax.optimization_barrier((pack("near", far[0])[0], gots[0]))
        gots.append(exchange(near, half, axis_index_groups=halves))
    else:
        parts = ("all",)
        gots = [exchange(pack("all")[0], peers)]
    base1 = jnp.dot(first_activations, value_weight_base, preferred_element_type=F32)
    base2 = jnp.dot(second_activations, value_weight_base, preferred_element_type=F32)
    pieces = (1 + 2 * plan.full + plan.rest) * len(gots)
    reply = pl.pallas_call(
        functools.partial(home_kernel, plan, parts),
        out_shape=jax.ShapeDtypeStruct((plan.packed, plan.ret_cols), BF16),
        in_specs=[vmem, vmem] + [anywhere] * len(gots),
        out_specs=anywhere,
        scratch_shapes=[
            pltpu.VMEM((plan.packed, plan.cols), BF16),
            pltpu.VMEM((plan.packed, plan.ret_cols), BF16),
            pltpu.SemaphoreType.DMA((pieces,)),
            pltpu.SemaphoreType.DMA((2,)),
        ],
        compiler_params=params,
        name="home",
    )(
        down.reshape(plan.joined, width),
        adapter_up_factors.reshape(plan.joined, feature),
        *gots,
    )
    out1, out2, resident_down, resident_up = pl.pallas_call(
        functools.partial(final_kernel, plan),
        out_shape=[
            jax.ShapeDtypeStruct((tok, feature), BF16),
            jax.ShapeDtypeStruct((tok, feature), BF16),
            jax.ShapeDtypeStruct((1, rank, width), BF16),
            jax.ShapeDtypeStruct((1, rank, feature), BF16),
        ],
        in_specs=[vmem, vmem, smem, vmem, vmem, vmem],
        out_specs=[vmem] * 4,
        compiler_params=params,
        name="finish",
    )(ids1, ids2, valid_row_counts, exchange(reply, peers), base1, base2)
    return out1, out2, jnp.swapaxes(resident_down, 1, 2), resident_up


def solution(mesh):
    return jax.shard_map(
        local,
        mesh=mesh,
        in_specs=(
            P(("groups", "replica"), None),
            P(("groups", "replica"), None),
            P(("groups", "replica")),
            P(("groups", "replica")),
            P(None, ("groups", "replica")),
            P("groups"),
            P(("groups", "replica")),
            P(),
            P("replica", None, None),
            P("replica", None, None),
        ),
        out_specs=(
            P(("groups", "replica"), None),
            P(("groups", "replica"), None),
            P(("groups", "replica"), None, None),
            P(("groups", "replica"), None, None),
        ),
        check_vma=False,
    )
```

```python
import functools

import jax
import jax.numpy as jnp
from jax import lax
from jax.experimental import pallas as pl
from jax.experimental.pallas import tpu as pltpu
from jax.sharding import PartitionSpec as P

LANES = 128
ROWS = 16
CHUNK = 256
F32 = jnp.float32
BF16 = jnp.bfloat16
NT = (((1,), (1,)), ((), ()))


class Plan:
    def __init__(self, peers, tok, width, rank, feature, homed):
        self.peers, self.tok, self.width, self.rank = peers, tok, width, rank
        self.feature, self.homed = feature, homed
        self.cap = max(2, 3 * tok // (2 * peers))
        combined = 2 * self.cap
        self.full = combined // ROWS
        left = combined - self.full * ROWS
        if left > 8:
            self.full, left = self.full + 1, 0
        self.rest = left > 0
        self.sections = self.full + self.rest
        self.packed = peers * ROWS
        self.joined = homed * rank
        self.tok_cols = self.full * width + self.rest * (width // 2)
        self.back_cols = self.full * feature + self.rest * (feature // 2)
        self.col_tiles = (width + feature) // LANES
        tiles = (rank // ROWS) * self.col_tiles
        share = -(-tiles // peers)
        while self.col_tiles % share:
            share += 1
        self.per_group = self.col_tiles // share
        self.holders = tiles // share
        self.spread = share * LANES
        self.meta_at = self.tok_cols + self.spread
        self.cols = self.meta_at + LANES
        self.ret_cols = self.spread + self.back_cols

    def row_chunks(self, count):
        size = min(CHUNK, count * ROWS)
        return [(i, size) for i in range(0, count * ROWS, size)]


def route(ids, homed):
    n = ids.shape[1]
    ids = jnp.broadcast_to(ids, (n, n))
    peer_row = ids // homed
    peer_col = jnp.transpose(ids.astype(F32)).astype(jnp.int32) // homed
    same = peer_row == peer_col
    above = lax.broadcasted_iota(jnp.int32, (n, n), 0)
    along = lax.broadcasted_iota(jnp.int32, (n, n), 1)
    pos_row = jnp.sum(jnp.where(same & (above < along), 1, 0), axis=0, keepdims=True)
    pos_col = jnp.sum(jnp.where(same & (along < above), 1, 0), axis=1, keepdims=True)
    return peer_row[0:1, :], pos_row, peer_col[:, 0:1], pos_col


def as_hot(mask):
    return jnp.where(mask, 1.0, 0.0).astype(BF16)


def pack_kernel(plan, ids1, ids2, popular, hosting, x1, x2, down, up, out, *scratch):
    ids, hot_ids, host_id, x, hot, packed, sems, out_sems = scratch
    me = lax.axis_index("replica")
    count = plan.peers
    quarter = plan.width // 4
    loads = [
        pltpu.make_async_copy(popular, hot_ids, sems.at[0]),
        pltpu.make_async_copy(hosting, host_id, sems.at[1]),
        pltpu.make_async_copy(ids1, ids.at[0], sems.at[2]),
        pltpu.make_async_copy(ids2, ids.at[1], sems.at[3]),
    ]
    for c in range(4):
        cols = pl.ds(c * quarter, quarter)
        for b, src in enumerate((x1, x2)):
            loads.append(
                pltpu.make_async_copy(
                    src.at[:, cols],
                    x.at[pl.ds(b * plan.tok, plan.tok), cols],
                    sems.at[4 + 2 * c + b],
                )
            )
    for load in loads:
        load.start()
    loads[0].wait()
    loads[1].wait()
    slot = jnp.int32(0)
    for i in range(hot_ids.shape[0]):
        adapter = hot_ids[i]
        slot = jnp.where(adapter // plan.homed == me, adapter % plan.homed, slot)
    wanted = hot_ids[host_id[0]] // plan.homed
    hots = [
        pltpu.make_async_copy(down.at[slot], hot.at[:, pl.ds(0, plan.width)], sems.at[12]),
        pltpu.make_async_copy(up.at[slot], hot.at[:, pl.ds(plan.width, plan.feature)], sems.at[13]),
    ]
    for load in hots:
        load.start()
    loads[2].wait()
    loads[3].wait()
    peers, cells, slots = [], [], []
    for b in range(2):
        peer, pos, _, _ = route(ids[b], plan.homed)
        peers.append(peer)
        cells.append(pos + b * plan.cap)
        slots.append((ids[b] % plan.homed).astype(F32))
    peer, cell = jnp.concatenate(peers, axis=1), jnp.concatenate(cells, axis=1)
    slots = jnp.concatenate(slots, axis=1)
    chunks = plan.row_chunks(count)
    stores = []

    def send(at, size):
        cols = pl.ds(at, size)
        stores.append(
            pltpu.make_async_copy(packed.at[:, cols], out.at[:, cols], out_sems.at[len(stores)])
        )
        stores[-1].start()

    masks = []
    for start, size in chunks:
        index = lax.broadcasted_iota(jnp.int32, (size, 2 * plan.tok), 0) + start
        own = index // ROWS == peer
        inner = index % ROWS
        sets = [own & (inner + s * ROWS == cell) for s in range(plan.full)]
        marks = list(sets)
        if plan.rest:
            low = own & (inner + plan.full * ROWS == cell) & (inner < 8)
            high = own & (inner - 8 + plan.full * ROWS == cell) & (inner >= 8)
            sets += [low, high]
            marks.append(low | high)
        masks.append([as_hot(m) for m in sets])
        lane = lax.broadcasted_iota(jnp.int32, (size, LANES), 1)
        meta = jnp.where(lane == plan.sections, wanted.astype(F32), 0.0)
        for s, mark in enumerate(marks):
            value = jnp.sum(jnp.where(mark, slots, 0.0), axis=1, keepdims=True)
            meta = jnp.where(lane == s, value, meta)
        packed[start : start + size, plan.meta_at :] = meta.astype(BF16)

    for c in range(4):
        loads[4 + 2 * c].wait()
        loads[5 + 2 * c].wait()
        cols = slice(c * quarter, (c + 1) * quarter)
        for (start, size), hot_masks in zip(chunks, masks):
            for s in range(plan.full):
                value = jnp.dot(hot_masks[s], x[:, cols], preferred_element_type=F32)
                at = s * plan.width + c * quarter
                packed[start : start + size, at : at + quarter] = value.astype(BF16)
        for s in range(plan.full):
            send(s * plan.width + c * quarter, quarter)
    if plan.rest:
        at = plan.full * plan.width
        for c in range(2):
            for (start, size), hot_masks in zip(chunks, masks):
                both = jnp.concatenate(hot_masks[plan.full :], axis=1)
                source = jnp.concatenate(
                    [
                        x[:, c * quarter : (c + 1) * quarter],
                        x[:, (c + 2) * quarter : (c + 3) * quarter],
                    ],
                    axis=0,
                )
                value = jnp.dot(both, source, preferred_element_type=F32)
                packed[start : start + size, at + c * quarter : at + (c + 1) * quarter] = (
                    value.astype(BF16)
                )
            send(at + c * quarter, quarter)
    for load in hots:
        load.wait()
    for i in range(count):
        group, col = divmod(i % plan.holders, plan.per_group)
        col *= plan.spread
        packed[i * ROWS : (i + 1) * ROWS, plan.tok_cols : plan.meta_at] = hot[
            group * ROWS : (group + 1) * ROWS, col : col + plan.spread
        ]
    send(plan.tok_cols, plan.spread + LANES)
    for store in stores:
        store.wait()


def home_kernel(plan, down, up, source, out, got, reply, sems, out_sems):
    bounds = [(plan.tok_cols, plan.spread + LANES)]
    bounds += [(c, plan.width // 2) for c in range(0, plan.tok_cols, plan.width // 2)]
    loads = []
    for at, size in bounds:
        cols = pl.ds(at, size)
        loads.append(
            pltpu.make_async_copy(source.at[:, cols], got.at[:, cols], sems.at[len(loads)])
        )
        loads[-1].start()

    def ready(i):
        loads[i].wait()

    chunks = plan.row_chunks(plan.peers)
    ready(0)
    metas = []
    for start, n in chunks:
        rows = slice(start, start + n)
        meta = got[rows, plan.meta_at :].astype(F32).astype(jnp.int32)
        metas.append(meta)
        wide = lax.broadcasted_iota(jnp.int32, (n, plan.packed), 1)
        inner = lax.broadcasted_iota(jnp.int32, (n, plan.packed), 0) % ROWS
        pick = as_hot(wide == meta[:, plan.sections : plan.sections + 1] * ROWS + inner)
        reply[rows, : plan.spread] = jnp.dot(
            pick, got[:, plan.tok_cols : plan.meta_at], preferred_element_type=F32
        ).astype(BF16)
    relayed = pltpu.make_async_copy(
        reply.at[:, pl.ds(0, plan.spread)], out.at[:, pl.ds(0, plan.spread)], out_sems.at[0]
    )
    relayed.start()
    half = plan.width // 2
    group = plan.joined
    for s in range(plan.sections):
        at = s * plan.width
        split = s == plan.full
        ready(1 + 2 * s)
        for i, ((start, n), meta) in enumerate(zip(chunks, metas)):
            rows = slice(start, start + n)
            low = lax.dot_general(
                got[rows, at : at + half], down[:, :half], NT, preferred_element_type=F32
            )
            if not split:
                if i == 0:
                    ready(2 + 2 * s)
                low += lax.dot_general(
                    got[rows, at + half : at + plan.width],
                    down[:, half:],
                    NT,
                    preferred_element_type=F32,
                )
                slot = meta[:, s : s + 1]
            else:
                high = lax.dot_general(
                    got[rows, at : at + half], down[:, half:], NT, preferred_element_type=F32
                )
                low = low.reshape(n // ROWS, 2, 8, group)[:, 0]
                high = high.reshape(n // ROWS, 2, 8, group)[:, 1]
                low = (low + high).reshape(n // 2, group)
                slot = meta.reshape(n // ROWS, 2, 8, LANES)[:, 0].reshape(n // 2, LANES)
                slot = slot[:, s : s + 1]
            column = lax.broadcasted_iota(jnp.int32, low.shape, 1) // plan.rank
            kept = jnp.where(column == slot, low, 0.0).astype(BF16)
            delta = jnp.dot(kept, up[...], preferred_element_type=F32)
            to = plan.spread + s * plan.feature
            if split:
                delta = delta.reshape(n // ROWS, 8, plan.feature)
                middle = plan.feature // 2
                delta = jnp.concatenate([delta[..., :middle], delta[..., middle:]], axis=1)
                delta = delta.reshape(n, middle)
            reply[rows, to : to + delta.shape[1]] = delta.astype(BF16)
    answered = pltpu.make_async_copy(
        reply.at[:, pl.ds(plan.spread, plan.back_cols)],
        out.at[:, pl.ds(plan.spread, plan.back_cols)],
        out_sems.at[1],
    )
    answered.start()
    relayed.wait()
    answered.wait()


def final_kernel(plan, ids1, ids2, counts, back, base1, base2, out1, out2, down, up):
    for d in range(plan.holders):
        rows = slice((d // plan.per_group) * ROWS, (d // plan.per_group + 1) * ROWS)
        for j in range(0, plan.spread, LANES):
            col = (d % plan.per_group) * plan.spread + j
            tile = back[d * ROWS : (d + 1) * ROWS, j : j + LANES]
            if col < plan.width:
                down[0, rows, col : col + LANES] = tile
            else:
                up[0, rows, col - plan.width : col - plan.width + LANES] = tile
    index = lax.broadcasted_iota(jnp.int32, (plan.tok, plan.packed), 1)
    inner = index % ROWS
    middle = plan.feature // 2
    for b, (ids, base, out) in enumerate(((ids1, base1, out1), (ids2, base2, out2))):
        _, _, peer, pos = route(ids[...], plan.homed)
        cell = pos + b * plan.cap
        own = index // ROWS == peer
        total = base[...]
        for s in range(plan.full):
            if (b + 1) * plan.cap <= s * ROWS or b * plan.cap >= (s + 1) * ROWS:
                continue
            hot = as_hot(own & (inner + s * ROWS == cell))
            at = plan.spread + s * plan.feature
            total += jnp.dot(hot, back[:, at : at + plan.feature], preferred_element_type=F32)
        if plan.rest and (b + 1) * plan.cap > plan.full * ROWS:
            at = plan.spread + plan.full * plan.feature
            values = back[:, at : at + middle]
            low = as_hot(own & (inner + plan.full * ROWS == cell) & (inner < 8))
            high = as_hot(own & (inner - 8 + plan.full * ROWS == cell) & (inner >= 8))
            total += jnp.concatenate(
                [jnp.dot(hot, values, preferred_element_type=F32) for hot in (low, high)], axis=1
            )
        valid = lax.broadcasted_iota(jnp.int32, total.shape, 0) < counts[b, 0]
        out[...] = jnp.where(valid, total, 0.0).astype(BF16)


class Wide:
    def __init__(self, plan, groups):
        self.peers, self.tok, self.width, self.rank = plan.peers, plan.tok, plan.width, plan.rank
        self.feature, self.homed, self.groups = plan.feature, plan.homed, groups
        self.half = self.peers // 2
        self.per = 2 * plan.cap
        self.sections = -(-2 * self.per // ROWS)
        self.packed = self.half * ROWS
        self.tok_cols = self.sections * self.width
        self.factor = self.width + self.feature
        col_tiles = self.factor // LANES
        tiles = (self.rank // ROWS) * col_tiles
        self.share = tiles // max(self.half, 1)
        self.spread = self.share * LANES
        self.meta_at = self.tok_cols + self.spread
        self.cols = self.meta_at + LANES
        self.back_cols = self.sections * self.feature
        self.ret_cols = self.back_cols + self.spread
        self.per_group = col_tiles // max(self.share, 1)
        self.cut = self.rank // 2
        self.fits = (
            groups == 2
            and self.half > 0
            and self.peers & (self.peers - 1) == 0
            and self.peers <= 16
            and tiles % self.half == 0
            and self.share > 0
            and col_tiles % self.share == 0
            and self.homed > 2
            and self.cut % ROWS == 0
        )

    def chunks(self, group):
        return [(a, group) for a in range(self.homed)] + [(self.homed - 1, 1 - group)]

    def place(self, j):
        group, col = divmod(j, self.per_group)
        return group * ROWS, col * self.spread


def cut_kernel(plan, popular, other, down, up, *refs):
    outs, (hot_ids, hot_sems, sems) = refs[:-3], refs[-3:]
    me, group = lax.axis_index("replica"), lax.axis_index("groups")
    order = travel_order(plan, me, popular, other, hot_ids, hot_sems)
    copies = []
    for (place, part), out in zip(plan.chunks(group), outs):
        rows = pl.ds(pl.multiple_of(part * plan.cut, ROWS), plan.cut)
        for src, cols in (
            (down, pl.ds(0, plan.width)),
            (up, pl.ds(plan.width, plan.feature)),
        ):
            copies.append(
                pltpu.make_async_copy(
                    src.at[order[place], rows], out.at[:, cols], sems.at[len(copies)]
                )
            )
    for copy in copies:
        copy.start()
    for copy in copies:
        copy.wait()


def travel_order(plan, home, popular, other, hot_ids, sems):
    loads = [
        pltpu.make_async_copy(src, hot_ids.at[i], sems.at[i])
        for i, src in enumerate((popular, other))
    ]
    for load in loads:
        load.start()
    for load in loads:
        load.wait()
    cold = [jnp.int32(1)] * plan.homed
    for g in range(2):
        for i in range(hot_ids.shape[1]):
            for a in range(plan.homed):
                cold[a] = jnp.where(hot_ids[g, i] == home * plan.homed + a, 0, cold[a])
    order = [jnp.int32(0)] * plan.homed
    for a in range(plan.homed):
        rank = jnp.int32(0)
        for b in range(plan.homed):
            if b != a:
                ahead = cold[b] <= cold[a] if b < a else cold[b] < cold[a]
                rank = rank + jnp.where(ahead, 1, 0)
        for c in range(plan.homed):
            order[c] = jnp.where(rank == c, a, order[c])
    return order


def mirror_of(plan, me):
    return me + plan.half - 2 * plan.half * (me // plan.half)


def hot_slot(popular, homed, home):
    slot = jnp.int32(0)
    for i in range(popular.shape[0]):
        adapter = popular[i]
        slot = jnp.where(adapter // homed == home, adapter % homed, slot)
    return slot


def near_pack_kernel(plan, ids1, ids2, popular, hosting, x1, x2, down, up, out, *scratch):
    ids, hot_ids, host_id, x, packed, sems, out_sems, hot_sems = scratch
    me = lax.axis_index("replica")
    side = me // plan.half
    quarter = plan.width // 4
    loads = [
        pltpu.make_async_copy(popular, hot_ids, sems.at[0]),
        pltpu.make_async_copy(hosting, host_id, sems.at[1]),
        pltpu.make_async_copy(ids1, ids.at[0], sems.at[2]),
        pltpu.make_async_copy(ids2, ids.at[1], sems.at[3]),
    ]
    for c in range(4):
        cols = pl.ds(c * quarter, quarter)
        for b, src in enumerate((x1, x2)):
            loads.append(
                pltpu.make_async_copy(
                    src.at[:, cols],
                    x.at[pl.ds(b * plan.tok, plan.tok), cols],
                    sems.at[4 + 2 * c + b],
                )
            )
    for load in loads:
        load.start()
    for load in loads[:4]:
        load.wait()
    slot = hot_slot(hot_ids, plan.homed, me)
    hots = []
    for j in range(plan.half):
        row, col = plan.place(j)
        rows, to = pl.ds(row, ROWS), pl.ds(j * ROWS, ROWS)
        inside = min(plan.spread, max(plan.width - col, 0))
        if inside:
            hots.append((down.at[slot, rows, pl.ds(col, inside)], to, 0, inside))
        if inside < plan.spread:
            from_up = pl.ds(col + inside - plan.width, plan.spread - inside)
            hots.append((up.at[slot, rows, from_up], to, inside, plan.spread - inside))
    stores = []
    for i, (src, to, at, size) in enumerate(hots):
        hots[i] = pltpu.make_async_copy(
            src, packed.at[to, pl.ds(plan.tok_cols + at, size)], hot_sems.at[i]
        )
        hots[i].start()
    wanted = hot_ids[host_id[0]] // plan.homed
    wanted = wanted % plan.half + jnp.where(wanted // plan.half == side, 0, plan.half)
    peers, cells, slots = [], [], []
    for b in range(2):
        home = ids[b] // plan.homed
        peer, pos, _, _ = route(home % plan.half, 1)
        peers.append(peer)
        cells.append(pos + b * plan.per)
        far = jnp.where(home // plan.half == side, 0, plan.homed)
        slots.append((ids[b] % plan.homed + far).astype(F32))
    peer, cell = jnp.concatenate(peers, axis=1), jnp.concatenate(cells, axis=1)
    slots = jnp.concatenate(slots, axis=1)
    index = lax.broadcasted_iota(jnp.int32, (plan.packed, 2 * plan.tok), 0)
    own = index // ROWS == peer
    inner = index % ROWS
    lane = lax.broadcasted_iota(jnp.int32, (plan.packed, LANES), 1)
    meta = jnp.where(lane == plan.sections, wanted.astype(F32), 0.0)
    masks = []
    for s in range(plan.sections):
        mark = own & (inner + s * ROWS == cell)
        masks.append(as_hot(mark))
        value = jnp.sum(jnp.where(mark, slots, 0.0), axis=1, keepdims=True)
        meta = jnp.where(lane == s, value, meta)
    mask = jnp.concatenate(masks, axis=0)
    packed[:, plan.meta_at :] = meta.astype(BF16)

    def send(at, size):
        stores.append(
            pltpu.make_async_copy(
                packed.at[:, pl.ds(at, size)],
                out.at[:, pl.ds(at, size)],
                out_sems.at[len(stores)],
            )
        )
        stores[-1].start()

    for c in range(4):
        loads[4 + 2 * c].wait()
        loads[5 + 2 * c].wait()
        value = jnp.dot(
            mask, x[:, c * quarter : (c + 1) * quarter], preferred_element_type=F32
        ).astype(BF16)
        for s in range(plan.sections):
            at = s * plan.width + c * quarter
            packed[:, at : at + quarter] = value[s * plan.packed : (s + 1) * plan.packed]
            send(at, quarter)
        if c == 0:
            for load in hots:
                load.wait()
            send(plan.tok_cols, plan.spread + LANES)
    for store in stores:
        store.wait()


def near_home_kernel(plan, got, popular, other, down, up, *refs):
    count = plan.homed
    arrays, out = refs[: 2 * count], refs[2 * count]
    x, meta, weights, ups, hot_ids, sems, hot_sems = refs[2 * count + 1 :]
    group = lax.axis_index("groups")
    pieces, joined = 4, plan.homed * plan.rank
    size = plan.width // pieces
    used = []

    def load(src, dst):
        used.append(pltpu.make_async_copy(src, dst, sems.at[len(used)]))
        used[-1].start()
        return used[-1]

    order = travel_order(
        plan, mirror_of(plan, lax.axis_index("replica")), popular, other, hot_ids, hot_sems
    )
    first = [load(got.at[:, pl.ds(plan.meta_at, LANES)], meta)]
    far = []
    halves = plan.chunks(group) + plan.chunks(1 - group)[: count - 1]
    for (place, part), array in zip(halves, arrays):
        at = joined + order[place] * plan.rank + part * plan.cut
        far.append((array, pl.ds(pl.multiple_of(at, ROWS), plan.cut)))
    steps = []
    for c in range(pieces):
        cols = pl.ds(c * size, size)
        step = []
        for s in range(plan.sections):
            step.append(
                load(
                    got.at[:, pl.ds(s * plan.width + c * size, size)],
                    x.at[pl.ds(s * plan.packed, plan.packed), cols],
                )
            )
        step.append(load(down.at[:, cols], weights.at[pl.ds(0, joined), cols]))
        for array, rows in far:
            step.append(load(array.at[:, cols], weights.at[rows, cols]))
        steps.append(step)
    first.append(load(up, ups.at[pl.ds(0, joined)]))
    for array, rows in far:
        first.append(load(array.at[:, pl.ds(plan.width, plan.feature)], ups.at[rows]))
    total = None
    for c, step in enumerate(steps):
        for copy in step:
            copy.wait()
        cols = slice(c * size, (c + 1) * size)
        term = lax.dot_general(x[:, cols], weights[:, cols], NT, preferred_element_type=F32)
        total = term if total is None else total + term
    for copy in first:
        copy.wait()
    slots = meta[...].astype(F32).astype(jnp.int32)
    slots = jnp.concatenate([slots[:, s : s + 1] for s in range(plan.sections)], axis=0)
    column = lax.broadcasted_iota(jnp.int32, total.shape, 1) // plan.rank
    kept = jnp.where(column == slots, total, 0.0).astype(BF16)
    delta = jnp.dot(kept, ups[...], preferred_element_type=F32).astype(BF16)
    for s in range(plan.sections):
        out[:, s * plan.feature : (s + 1) * plan.feature] = delta[
            s * plan.packed : (s + 1) * plan.packed
        ]


def far_hot_kernel(plan, popular, other, *refs):
    out, hot_ids, hot_sems, sems = refs[-4:]
    count = 2
    crossed, swapped = refs[:count], refs[count : 2 * count]
    mirror = mirror_of(plan, lax.axis_index("replica"))
    group = lax.axis_index("groups")
    order = travel_order(plan, mirror, popular, other, hot_ids, hot_sems)
    second = hot_slot(hot_ids.at[0], plan.homed, mirror) == order[1]
    for place in range(2):
        for g in range(2):

            @pl.when((second if place else ~second) & (group == g))
            def _():
                copies = []
                for j in range(plan.half):
                    row, col = plan.place(j)
                    part, row = divmod(row, plan.cut)
                    src = (crossed if part == g else swapped)[place]
                    copies.append(
                        pltpu.make_async_copy(
                            src.at[pl.ds(row, ROWS), pl.ds(col, plan.spread)],
                            out.at[pl.ds(j * ROWS, ROWS)],
                            sems.at[j],
                        )
                    )
                    copies[-1].start()
                for copy in copies:
                    copy.wait()


def relay_kernel(plan, got, far, reply, out, held, meta, sems):
    copies = [
        pltpu.make_async_copy(got.at[:, pl.ds(plan.meta_at, LANES)], meta, sems.at[0]),
        pltpu.make_async_copy(
            got.at[:, pl.ds(plan.tok_cols, plan.spread)],
            held.at[pl.ds(0, plan.packed)],
            sems.at[1],
        ),
        pltpu.make_async_copy(far, held.at[pl.ds(plan.packed, plan.packed)], sems.at[2]),
        pltpu.make_async_copy(reply, out.at[:, pl.ds(0, plan.back_cols)], sems.at[3]),
    ]
    for copy in copies:
        copy.start()
    for copy in copies[:3]:
        copy.wait()
    wanted = meta[...].astype(F32).astype(jnp.int32)[:, plan.sections : plan.sections + 1]
    shape = (plan.packed, 2 * plan.packed)
    inner = lax.broadcasted_iota(jnp.int32, shape, 0) % ROWS
    pick = as_hot(lax.broadcasted_iota(jnp.int32, shape, 1) == wanted * ROWS + inner)
    out[:, plan.back_cols :] = jnp.dot(
        pick, held[...], preferred_element_type=F32
    ).astype(BF16)
    copies[3].wait()


def near_final_kernel(plan, ids1, ids2, counts, back, base1, base2, out1, out2, down, up):
    for j in range(plan.half):
        row, first = plan.place(j)
        rows = slice(row, row + ROWS)
        for at in range(0, plan.spread, LANES):
            col = first + at
            start = plan.back_cols + at
            tile = back[j * ROWS : (j + 1) * ROWS, start : start + LANES]
            if col < plan.width:
                down[0, rows, col : col + LANES] = tile
            else:
                up[0, rows, col - plan.width : col - plan.width + LANES] = tile
    index = lax.broadcasted_iota(jnp.int32, (plan.tok, plan.packed), 1)
    inner = index % ROWS
    for b, (ids, base, out) in enumerate(((ids1, base1, out1), (ids2, base2, out2))):
        _, _, peer, pos = route((ids[...] // plan.homed) % plan.half, 1)
        cell = pos + b * plan.per
        own = index // ROWS == peer
        total = base[...]
        for s in range(plan.sections):
            if (b + 1) * plan.per <= s * ROWS or b * plan.per >= (s + 1) * ROWS:
                continue
            hot = as_hot(own & (inner + s * ROWS == cell))
            at = s * plan.feature
            total += jnp.dot(hot, back[:, at : at + plan.feature], preferred_element_type=F32)
        valid = lax.broadcasted_iota(jnp.int32, total.shape, 0) < counts[b, 0]
        out[...] = jnp.where(valid, total, 0.0).astype(BF16)


def call(kernel, name, out_shape, operands, in_specs, out_specs, scratch=(), cost=0):
    return pl.pallas_call(
        kernel,
        out_shape=out_shape,
        in_specs=in_specs,
        out_specs=out_specs,
        scratch_shapes=list(scratch),
        compiler_params=pltpu.CompilerParams(vmem_limit_bytes=60 * 1024 * 1024),
        cost_estimate=pl.CostEstimate(flops=0, bytes_accessed=cost, transcendentals=0)
        if cost
        else None,
        name=name,
    )(*operands)


def exchange(x, n, **kwargs):
    x = x.reshape(n, x.shape[0] // n, x.shape[1])
    x = lax.all_to_all(x, "replica", split_axis=0, concat_axis=0, tiled=True, **kwargs)
    return x.reshape(n * x.shape[1], x.shape[2])


def local(
    first_activations,
    second_activations,
    first_adapter_ids,
    second_adapter_ids,
    valid_row_counts,
    popular_adapters,
    replica_hosting,
    value_weight_base,
    adapter_down_factors,
    adapter_up_factors,
):
    tok, width = first_activations.shape
    homed, _, rank = adapter_down_factors.shape
    feature = adapter_up_factors.shape[2]
    plan = Plan(lax.axis_size("replica"), tok, width, rank, feature, homed)
    wide = Wide(plan, lax.axis_size("groups"))
    down = jnp.swapaxes(adapter_down_factors, 1, 2)
    up = adapter_up_factors
    ids1 = first_adapter_ids.reshape(1, tok)
    ids2 = second_adapter_ids.reshape(1, tok)
    anywhere = pl.BlockSpec(memory_space=pl.ANY)
    vmem = pl.BlockSpec(memory_space=pltpu.VMEM)
    smem = pl.BlockSpec(memory_space=pltpu.SMEM)
    dma = pltpu.SemaphoreType.DMA
    sources = (
        ids1,
        ids2,
        popular_adapters,
        replica_hosting,
        first_activations,
        second_activations,
        down,
        up,
    )
    first_scratch = [
        pltpu.VMEM((2, 1, tok), jnp.int32),
        pltpu.SMEM(popular_adapters.shape, jnp.int32),
        pltpu.SMEM(replica_hosting.shape, jnp.int32),
        pltpu.VMEM((2 * tok, width), BF16),
    ]
    base1 = jnp.dot(first_activations, value_weight_base, preferred_element_type=F32)
    base2 = jnp.dot(second_activations, value_weight_base, preferred_element_type=F32)
    down_joined, up_joined = down.reshape(homed * rank, width), up.reshape(homed * rank, feature)

    def shape(*dims):
        return jax.ShapeDtypeStruct(dims, BF16)

    if wide.fits:
        half = wide.half
        count = homed + 1
        halves = [list(range(half)), list(range(half, wide.peers))]
        across = [(0, 1), (1, 0)]
        mirror = [(i, i ^ half) for i in range(wide.peers)]
        other = lax.ppermute(popular_adapters, "groups", across)
        both_hot = pltpu.SMEM((2,) + popular_adapters.shape, jnp.int32)
        cuts = call(
            functools.partial(cut_kernel, wide),
            "cut",
            [shape(wide.cut, wide.factor)] * count,
            (popular_adapters, other, down, up),
            [anywhere] * 4,
            [vmem] * count,
            [both_hot, dma((2,)), dma((2 * count,))],
        )
        crossed = [lax.ppermute(c, "replica", mirror) for c in cuts]
        swapped = [lax.ppermute(c, "groups", across) for c in crossed[: homed - 1]]
        sent = call(
            functools.partial(near_pack_kernel, wide),
            "pack",
            shape(wide.packed, wide.cols),
            sources,
            [anywhere] * 8,
            anywhere,
            first_scratch
            + [
                pltpu.VMEM((wide.packed, wide.cols), BF16),
                dma((12,)),
                dma((4 * wide.sections + 1,)),
                dma((2 * half,)),
            ],
            cost=4 * wide.packed * wide.cols,
        )
        got = exchange(sent, half, axis_index_groups=halves)
        got, *arrived = lax.optimization_barrier((got, *crossed))
        hot = call(
            functools.partial(far_hot_kernel, wide),
            "far_hot",
            shape(wide.packed, wide.spread),
            (popular_adapters, other, *arrived[:2], *swapped),
            [anywhere] * (4 + homed - 1),
            vmem,
            [both_hot, dma((2,)), dma((half,))],
        )
        far = exchange(hot, half, axis_index_groups=halves)
        rows = 2 * homed * rank
        reply = call(
            functools.partial(near_home_kernel, wide),
            "home",
            shape(wide.packed, wide.back_cols),
            (got, popular_adapters, other, down_joined, up_joined, *crossed, *swapped),
            [anywhere] * (5 + 2 * homed),
            vmem,
            [
                pltpu.VMEM((wide.sections * wide.packed, width), BF16),
                pltpu.VMEM((wide.packed, LANES), BF16),
                pltpu.VMEM((rows, width), BF16),
                pltpu.VMEM((rows, feature), BF16),
                both_hot,
                dma((2 + 2 * homed + 4 * (wide.sections + 1 + 2 * homed),)),
                dma((2,)),
            ],
        )
        answer = call(
            functools.partial(relay_kernel, wide),
            "relay",
            shape(wide.packed, wide.ret_cols),
            (got, far, reply),
            [anywhere] * 3,
            vmem,
            [
                pltpu.VMEM((2 * wide.packed, wide.spread), BF16),
                pltpu.VMEM((wide.packed, LANES), BF16),
                dma((4,)),
            ],
        )
        back = exchange(answer, half, axis_index_groups=halves)
        finish = functools.partial(near_final_kernel, wide)
    else:
        sent = call(
            functools.partial(pack_kernel, plan),
            "pack",
            shape(plan.packed, plan.cols),
            sources,
            [anywhere] * 8,
            anywhere,
            first_scratch
            + [
                pltpu.VMEM((rank, width + feature), BF16),
                pltpu.VMEM((plan.packed, plan.cols), BF16),
                dma((14,)),
                dma((4 * plan.full + 2 * plan.rest + 1,)),
            ],
        )
        got = exchange(sent, plan.peers)
        reply = call(
            functools.partial(home_kernel, plan),
            "home",
            shape(plan.packed, plan.ret_cols),
            (down_joined, up_joined, got),
            [vmem, vmem, anywhere],
            anywhere,
            [
                pltpu.VMEM((plan.packed, plan.cols), BF16),
                pltpu.VMEM((plan.packed, plan.ret_cols), BF16),
                dma((1 + 2 * plan.full + plan.rest,)),
                dma((2,)),
            ],
        )
        back = exchange(reply, plan.peers)
        finish = functools.partial(final_kernel, plan)
    out1, out2, resident_down, resident_up = call(
        finish,
        "finish",
        [shape(tok, feature), shape(tok, feature), shape(1, rank, width), shape(1, rank, feature)],
        (ids1, ids2, valid_row_counts, back, base1, base2),
        [vmem, vmem, smem, vmem, vmem, vmem],
        [vmem] * 4,
    )
    return out1, out2, jnp.swapaxes(resident_down, 1, 2), resident_up


def solution(mesh):
    return jax.shard_map(
        local,
        mesh=mesh,
        in_specs=(
            P(("groups", "replica"), None),
            P(("groups", "replica"), None),
            P(("groups", "replica")),
            P(("groups", "replica")),
            P(None, ("groups", "replica")),
            P("groups"),
            P(("groups", "replica")),
            P(),
            P("replica", None, None),
            P("replica", None, None),
        ),
        out_specs=(
            P(("groups", "replica"), None),
            P(("groups", "replica"), None),
            P(("groups", "replica"), None, None),
            P(("groups", "replica"), None, None),
        ),
        check_vma=False,
    )
```

```python
import functools

import jax
import jax.numpy as jnp
from jax import lax
from jax.experimental import pallas as pl
from jax.experimental.pallas import tpu as pltpu
from jax.sharding import PartitionSpec as P

LANES = 128
ROWS = 16
CHUNK = 256
F32 = jnp.float32
BF16 = jnp.bfloat16
NT = (((1,), (1,)), ((), ()))


class Plan:
    def __init__(self, peers, tok, width, rank, feature, homed):
        self.peers, self.tok, self.width, self.rank = peers, tok, width, rank
        self.feature, self.homed = feature, homed
        self.cap = max(2, 3 * tok // (2 * peers))
        combined = 2 * self.cap
        self.full = combined // ROWS
        left = combined - self.full * ROWS
        if left > 8:
            self.full, left = self.full + 1, 0
        self.rest = left > 0
        self.sections = self.full + self.rest
        self.packed = peers * ROWS
        self.joined = homed * rank
        self.tok_cols = self.full * width + self.rest * (width // 2)
        self.back_cols = self.full * feature + self.rest * (feature // 2)
        self.col_tiles = (width + feature) // LANES
        tiles = (rank // ROWS) * self.col_tiles
        share = -(-tiles // peers)
        while self.col_tiles % share:
            share += 1
        self.per_group = self.col_tiles // share
        self.holders = tiles // share
        self.spread = share * LANES
        self.meta_at = self.tok_cols + self.spread
        self.cols = self.meta_at + LANES
        self.ret_cols = self.spread + self.back_cols

    def row_chunks(self, count):
        size = min(CHUNK, count * ROWS)
        return [(i, size) for i in range(0, count * ROWS, size)]


def route(ids, homed):
    n = ids.shape[1]
    ids = jnp.broadcast_to(ids, (n, n))
    peer_row = ids // homed
    peer_col = jnp.transpose(ids.astype(F32)).astype(jnp.int32) // homed
    same = peer_row == peer_col
    above = lax.broadcasted_iota(jnp.int32, (n, n), 0)
    along = lax.broadcasted_iota(jnp.int32, (n, n), 1)
    pos_row = jnp.sum(jnp.where(same & (above < along), 1, 0), axis=0, keepdims=True)
    pos_col = jnp.sum(jnp.where(same & (along < above), 1, 0), axis=1, keepdims=True)
    return peer_row[0:1, :], pos_row, peer_col[:, 0:1], pos_col


def as_hot(mask):
    return jnp.where(mask, 1.0, 0.0).astype(BF16)


def pack_kernel(plan, ids1, ids2, popular, hosting, x1, x2, down, up, out, *scratch):
    ids, hot_ids, host_id, x, hot, packed, sems, out_sems = scratch
    me = lax.axis_index("replica")
    count = plan.peers
    quarter = plan.width // 4
    loads = [
        pltpu.make_async_copy(popular, hot_ids, sems.at[0]),
        pltpu.make_async_copy(hosting, host_id, sems.at[1]),
        pltpu.make_async_copy(ids1, ids.at[0], sems.at[2]),
        pltpu.make_async_copy(ids2, ids.at[1], sems.at[3]),
    ]
    for c in range(4):
        cols = pl.ds(c * quarter, quarter)
        for b, src in enumerate((x1, x2)):
            loads.append(
                pltpu.make_async_copy(
                    src.at[:, cols],
                    x.at[pl.ds(b * plan.tok, plan.tok), cols],
                    sems.at[4 + 2 * c + b],
                )
            )
    for load in loads:
        load.start()
    loads[0].wait()
    loads[1].wait()
    slot = jnp.int32(0)
    for i in range(hot_ids.shape[0]):
        adapter = hot_ids[i]
        slot = jnp.where(adapter // plan.homed == me, adapter % plan.homed, slot)
    wanted = hot_ids[host_id[0]] // plan.homed
    hots = [
        pltpu.make_async_copy(down.at[slot], hot.at[:, pl.ds(0, plan.width)], sems.at[12]),
        pltpu.make_async_copy(up.at[slot], hot.at[:, pl.ds(plan.width, plan.feature)], sems.at[13]),
    ]
    for load in hots:
        load.start()
    loads[2].wait()
    loads[3].wait()
    peers, cells, slots = [], [], []
    for b in range(2):
        peer, pos, _, _ = route(ids[b], plan.homed)
        peers.append(peer)
        cells.append(pos + b * plan.cap)
        slots.append((ids[b] % plan.homed).astype(F32))
    peer, cell = jnp.concatenate(peers, axis=1), jnp.concatenate(cells, axis=1)
    slots = jnp.concatenate(slots, axis=1)
    chunks = plan.row_chunks(count)
    stores = []

    def send(at, size):
        cols = pl.ds(at, size)
        stores.append(
            pltpu.make_async_copy(packed.at[:, cols], out.at[:, cols], out_sems.at[len(stores)])
        )
        stores[-1].start()

    masks = []
    for start, size in chunks:
        index = lax.broadcasted_iota(jnp.int32, (size, 2 * plan.tok), 0) + start
        own = index // ROWS == peer
        inner = index % ROWS
        sets = [own & (inner + s * ROWS == cell) for s in range(plan.full)]
        marks = list(sets)
        if plan.rest:
            low = own & (inner + plan.full * ROWS == cell) & (inner < 8)
            high = own & (inner - 8 + plan.full * ROWS == cell) & (inner >= 8)
            sets += [low, high]
            marks.append(low | high)
        masks.append([as_hot(m) for m in sets])
        lane = lax.broadcasted_iota(jnp.int32, (size, LANES), 1)
        meta = jnp.where(lane == plan.sections, wanted.astype(F32), 0.0)
        for s, mark in enumerate(marks):
            value = jnp.sum(jnp.where(mark, slots, 0.0), axis=1, keepdims=True)
            meta = jnp.where(lane == s, value, meta)
        packed[start : start + size, plan.meta_at :] = meta.astype(BF16)

    for c in range(4):
        loads[4 + 2 * c].wait()
        loads[5 + 2 * c].wait()
        cols = slice(c * quarter, (c + 1) * quarter)
        for (start, size), hot_masks in zip(chunks, masks):
            for s in range(plan.full):
                value = jnp.dot(hot_masks[s], x[:, cols], preferred_element_type=F32)
                at = s * plan.width + c * quarter
                packed[start : start + size, at : at + quarter] = value.astype(BF16)
        for s in range(plan.full):
            send(s * plan.width + c * quarter, quarter)
    if plan.rest:
        at = plan.full * plan.width
        for c in range(2):
            for (start, size), hot_masks in zip(chunks, masks):
                both = jnp.concatenate(hot_masks[plan.full :], axis=1)
                source = jnp.concatenate(
                    [
                        x[:, c * quarter : (c + 1) * quarter],
                        x[:, (c + 2) * quarter : (c + 3) * quarter],
                    ],
                    axis=0,
                )
                value = jnp.dot(both, source, preferred_element_type=F32)
                packed[start : start + size, at + c * quarter : at + (c + 1) * quarter] = (
                    value.astype(BF16)
                )
            send(at + c * quarter, quarter)
    for load in hots:
        load.wait()
    for i in range(count):
        group, col = divmod(i % plan.holders, plan.per_group)
        col *= plan.spread
        packed[i * ROWS : (i + 1) * ROWS, plan.tok_cols : plan.meta_at] = hot[
            group * ROWS : (group + 1) * ROWS, col : col + plan.spread
        ]
    send(plan.tok_cols, plan.spread + LANES)
    for store in stores:
        store.wait()


def home_kernel(plan, down, up, source, out, got, reply, sems, out_sems):
    bounds = [(plan.tok_cols, plan.spread + LANES)]
    bounds += [(c, plan.width // 2) for c in range(0, plan.tok_cols, plan.width // 2)]
    loads = []
    for at, size in bounds:
        cols = pl.ds(at, size)
        loads.append(
            pltpu.make_async_copy(source.at[:, cols], got.at[:, cols], sems.at[len(loads)])
        )
        loads[-1].start()

    def ready(i):
        loads[i].wait()

    chunks = plan.row_chunks(plan.peers)
    ready(0)
    metas = []
    for start, n in chunks:
        rows = slice(start, start + n)
        meta = got[rows, plan.meta_at :].astype(F32).astype(jnp.int32)
        metas.append(meta)
        wide = lax.broadcasted_iota(jnp.int32, (n, plan.packed), 1)
        inner = lax.broadcasted_iota(jnp.int32, (n, plan.packed), 0) % ROWS
        pick = as_hot(wide == meta[:, plan.sections : plan.sections + 1] * ROWS + inner)
        reply[rows, : plan.spread] = jnp.dot(
            pick, got[:, plan.tok_cols : plan.meta_at], preferred_element_type=F32
        ).astype(BF16)
    relayed = pltpu.make_async_copy(
        reply.at[:, pl.ds(0, plan.spread)], out.at[:, pl.ds(0, plan.spread)], out_sems.at[0]
    )
    relayed.start()
    half = plan.width // 2
    group = plan.joined
    for s in range(plan.sections):
        at = s * plan.width
        split = s == plan.full
        ready(1 + 2 * s)
        for i, ((start, n), meta) in enumerate(zip(chunks, metas)):
            rows = slice(start, start + n)
            low = lax.dot_general(
                got[rows, at : at + half], down[:, :half], NT, preferred_element_type=F32
            )
            if not split:
                if i == 0:
                    ready(2 + 2 * s)
                low += lax.dot_general(
                    got[rows, at + half : at + plan.width],
                    down[:, half:],
                    NT,
                    preferred_element_type=F32,
                )
                slot = meta[:, s : s + 1]
            else:
                high = lax.dot_general(
                    got[rows, at : at + half], down[:, half:], NT, preferred_element_type=F32
                )
                low = low.reshape(n // ROWS, 2, 8, group)[:, 0]
                high = high.reshape(n // ROWS, 2, 8, group)[:, 1]
                low = (low + high).reshape(n // 2, group)
                slot = meta.reshape(n // ROWS, 2, 8, LANES)[:, 0].reshape(n // 2, LANES)
                slot = slot[:, s : s + 1]
            column = lax.broadcasted_iota(jnp.int32, low.shape, 1) // plan.rank
            kept = jnp.where(column == slot, low, 0.0).astype(BF16)
            delta = jnp.dot(kept, up[...], preferred_element_type=F32)
            to = plan.spread + s * plan.feature
            if split:
                delta = delta.reshape(n // ROWS, 8, plan.feature)
                middle = plan.feature // 2
                delta = jnp.concatenate([delta[..., :middle], delta[..., middle:]], axis=1)
                delta = delta.reshape(n, middle)
            reply[rows, to : to + delta.shape[1]] = delta.astype(BF16)
    answered = pltpu.make_async_copy(
        reply.at[:, pl.ds(plan.spread, plan.back_cols)],
        out.at[:, pl.ds(plan.spread, plan.back_cols)],
        out_sems.at[1],
    )
    answered.start()
    relayed.wait()
    answered.wait()


def final_kernel(plan, ids1, ids2, counts, back, base1, base2, out1, out2, down, up):
    for d in range(plan.holders):
        rows = slice((d // plan.per_group) * ROWS, (d // plan.per_group + 1) * ROWS)
        for j in range(0, plan.spread, LANES):
            col = (d % plan.per_group) * plan.spread + j
            tile = back[d * ROWS : (d + 1) * ROWS, j : j + LANES]
            if col < plan.width:
                down[0, rows, col : col + LANES] = tile
            else:
                up[0, rows, col - plan.width : col - plan.width + LANES] = tile
    index = lax.broadcasted_iota(jnp.int32, (plan.tok, plan.packed), 1)
    inner = index % ROWS
    middle = plan.feature // 2
    for b, (ids, base, out) in enumerate(((ids1, base1, out1), (ids2, base2, out2))):
        _, _, peer, pos = route(ids[...], plan.homed)
        cell = pos + b * plan.cap
        own = index // ROWS == peer
        total = base[...]
        for s in range(plan.full):
            if (b + 1) * plan.cap <= s * ROWS or b * plan.cap >= (s + 1) * ROWS:
                continue
            hot = as_hot(own & (inner + s * ROWS == cell))
            at = plan.spread + s * plan.feature
            total += jnp.dot(hot, back[:, at : at + plan.feature], preferred_element_type=F32)
        if plan.rest and (b + 1) * plan.cap > plan.full * ROWS:
            at = plan.spread + plan.full * plan.feature
            values = back[:, at : at + middle]
            low = as_hot(own & (inner + plan.full * ROWS == cell) & (inner < 8))
            high = as_hot(own & (inner - 8 + plan.full * ROWS == cell) & (inner >= 8))
            total += jnp.concatenate(
                [jnp.dot(hot, values, preferred_element_type=F32) for hot in (low, high)], axis=1
            )
        valid = lax.broadcasted_iota(jnp.int32, total.shape, 0) < counts[b, 0]
        out[...] = jnp.where(valid, total, 0.0).astype(BF16)


class Wide:
    def __init__(self, plan, groups):
        self.peers, self.tok, self.width, self.rank = plan.peers, plan.tok, plan.width, plan.rank
        self.feature, self.homed, self.groups = plan.feature, plan.homed, groups
        self.half = self.peers // 2
        self.per = 2 * plan.cap
        self.sections = -(-2 * self.per // ROWS)
        self.packed = self.half * ROWS
        self.tok_cols = self.sections * self.width
        self.factor = self.width + self.feature
        col_tiles = self.factor // LANES
        tiles = (self.rank // ROWS) * col_tiles
        self.share = tiles // max(self.half, 1)
        self.spread = self.share * LANES
        self.meta_at = self.tok_cols + self.spread
        self.cols = self.meta_at + LANES
        self.back_cols = self.sections * self.feature
        self.ret_cols = self.back_cols + self.spread
        self.per_group = col_tiles // max(self.share, 1)
        self.cut = self.rank // 2
        self.fits = (
            groups == 2
            and self.half > 0
            and self.peers & (self.peers - 1) == 0
            and self.peers <= 16
            and tiles % self.half == 0
            and self.share > 0
            and col_tiles % self.share == 0
            and self.cut % ROWS == 0
        )

    def chunks(self, group):
        return [(a, group) for a in range(self.homed)] + [(self.homed - 1, 1 - group)]

    def place(self, j):
        group, col = divmod(j, self.per_group)
        return group * ROWS, col * self.spread


def cut_kernel(plan, down, up, *refs):
    outs, sems = refs[:-1], refs[-1]
    copies = []
    for (adapter, part), out in zip(plan.chunks(lax.axis_index("groups")), outs):
        rows = pl.ds(pl.multiple_of(part * plan.cut, ROWS), plan.cut)
        for src, cols in (
            (down, pl.ds(0, plan.width)),
            (up, pl.ds(plan.width, plan.feature)),
        ):
            copies.append(
                pltpu.make_async_copy(
                    src.at[adapter, rows], out.at[:, cols], sems.at[len(copies)]
                )
            )
    for copy in copies:
        copy.start()
    for copy in copies:
        copy.wait()


def mirror_of(plan, me):
    return me + plan.half - 2 * plan.half * (me // plan.half)


def hot_slot(popular, homed, home):
    slot = jnp.int32(0)
    for i in range(popular.shape[0]):
        adapter = popular[i]
        slot = jnp.where(adapter // homed == home, adapter % homed, slot)
    return slot


def near_pack_kernel(plan, ids1, ids2, popular, hosting, x1, x2, down, up, out, *scratch):
    ids, hot_ids, host_id, x, packed, sems, out_sems, hot_sems = scratch
    me = lax.axis_index("replica")
    side = me // plan.half
    quarter = plan.width // 4
    loads = [
        pltpu.make_async_copy(popular, hot_ids, sems.at[0]),
        pltpu.make_async_copy(hosting, host_id, sems.at[1]),
        pltpu.make_async_copy(ids1, ids.at[0], sems.at[2]),
        pltpu.make_async_copy(ids2, ids.at[1], sems.at[3]),
    ]
    for c in range(4):
        cols = pl.ds(c * quarter, quarter)
        for b, src in enumerate((x1, x2)):
            loads.append(
                pltpu.make_async_copy(
                    src.at[:, cols],
                    x.at[pl.ds(b * plan.tok, plan.tok), cols],
                    sems.at[4 + 2 * c + b],
                )
            )
    for load in loads:
        load.start()
    for load in loads[:4]:
        load.wait()
    slot = hot_slot(hot_ids, plan.homed, me)
    hots = []
    for j in range(plan.half):
        row, col = plan.place(j)
        rows, to = pl.ds(row, ROWS), pl.ds(j * ROWS, ROWS)
        inside = min(plan.spread, max(plan.width - col, 0))
        if inside:
            hots.append((down.at[slot, rows, pl.ds(col, inside)], to, 0, inside))
        if inside < plan.spread:
            from_up = pl.ds(col + inside - plan.width, plan.spread - inside)
            hots.append((up.at[slot, rows, from_up], to, inside, plan.spread - inside))
    stores = []
    for i, (src, to, at, size) in enumerate(hots):
        hots[i] = pltpu.make_async_copy(
            src, packed.at[to, pl.ds(plan.tok_cols + at, size)], hot_sems.at[i]
        )
        hots[i].start()
    wanted = hot_ids[host_id[0]] // plan.homed
    wanted = wanted % plan.half + jnp.where(wanted // plan.half == side, 0, plan.half)
    peers, cells, slots = [], [], []
    for b in range(2):
        home = ids[b] // plan.homed
        peer, pos, _, _ = route(home % plan.half, 1)
        peers.append(peer)
        cells.append(pos + b * plan.per)
        far = jnp.where(home // plan.half == side, 0, plan.homed)
        slots.append((ids[b] % plan.homed + far).astype(F32))
    peer, cell = jnp.concatenate(peers, axis=1), jnp.concatenate(cells, axis=1)
    slots = jnp.concatenate(slots, axis=1)
    index = lax.broadcasted_iota(jnp.int32, (plan.packed, 2 * plan.tok), 0)
    own = index // ROWS == peer
    inner = index % ROWS
    lane = lax.broadcasted_iota(jnp.int32, (plan.packed, LANES), 1)
    meta = jnp.where(lane == plan.sections, wanted.astype(F32), 0.0)
    masks = []
    for s in range(plan.sections):
        mark = own & (inner + s * ROWS == cell)
        masks.append(as_hot(mark))
        value = jnp.sum(jnp.where(mark, slots, 0.0), axis=1, keepdims=True)
        meta = jnp.where(lane == s, value, meta)
    mask = jnp.concatenate(masks, axis=0)
    packed[:, plan.meta_at :] = meta.astype(BF16)

    def send(at, size):
        stores.append(
            pltpu.make_async_copy(
                packed.at[:, pl.ds(at, size)],
                out.at[:, pl.ds(at, size)],
                out_sems.at[len(stores)],
            )
        )
        stores[-1].start()

    for c in range(4):
        loads[4 + 2 * c].wait()
        loads[5 + 2 * c].wait()
        value = jnp.dot(
            mask, x[:, c * quarter : (c + 1) * quarter], preferred_element_type=F32
        ).astype(BF16)
        for s in range(plan.sections):
            at = s * plan.width + c * quarter
            packed[:, at : at + quarter] = value[s * plan.packed : (s + 1) * plan.packed]
            send(at, quarter)
        if c == 0:
            for load in hots:
                load.wait()
            send(plan.tok_cols, plan.spread + LANES)
    for store in stores:
        store.wait()


def near_home_kernel(plan, got, down, up, *refs):
    count = plan.homed
    arrays, out = refs[: 2 * count], refs[2 * count]
    x, meta, weights, ups, sems = refs[2 * count + 1 :]
    group = lax.axis_index("groups")
    pieces, joined = 4, plan.homed * plan.rank
    size = plan.width // pieces
    used = []

    def load(src, dst):
        used.append(pltpu.make_async_copy(src, dst, sems.at[len(used)]))
        used[-1].start()
        return used[-1]

    first = [load(got.at[:, pl.ds(plan.meta_at, LANES)], meta)]
    far = []
    halves = plan.chunks(group) + plan.chunks(1 - group)[: count - 1]
    for (adapter, part), array in zip(halves, arrays):
        at = joined + adapter * plan.rank + part * plan.cut
        far.append((array, pl.ds(pl.multiple_of(at, ROWS), plan.cut)))
    steps = []
    for c in range(pieces):
        cols = pl.ds(c * size, size)
        step = []
        for s in range(plan.sections):
            step.append(
                load(
                    got.at[:, pl.ds(s * plan.width + c * size, size)],
                    x.at[pl.ds(s * plan.packed, plan.packed), cols],
                )
            )
        step.append(load(down.at[:, cols], weights.at[pl.ds(0, joined), cols]))
        for array, rows in far:
            step.append(load(array.at[:, cols], weights.at[rows, cols]))
        steps.append(step)
    first.append(load(up, ups.at[pl.ds(0, joined)]))
    for array, rows in far:
        first.append(load(array.at[:, pl.ds(plan.width, plan.feature)], ups.at[rows]))
    total = None
    for c, step in enumerate(steps):
        for copy in step:
            copy.wait()
        cols = slice(c * size, (c + 1) * size)
        term = lax.dot_general(x[:, cols], weights[:, cols], NT, preferred_element_type=F32)
        total = term if total is None else total + term
    for copy in first:
        copy.wait()
    slots = meta[...].astype(F32).astype(jnp.int32)
    slots = jnp.concatenate([slots[:, s : s + 1] for s in range(plan.sections)], axis=0)
    column = lax.broadcasted_iota(jnp.int32, total.shape, 1) // plan.rank
    kept = jnp.where(column == slots, total, 0.0).astype(BF16)
    delta = jnp.dot(kept, ups[...], preferred_element_type=F32).astype(BF16)
    for s in range(plan.sections):
        out[:, s * plan.feature : (s + 1) * plan.feature] = delta[
            s * plan.packed : (s + 1) * plan.packed
        ]


def far_hot_kernel(plan, popular, *refs):
    count = plan.homed
    arrays, (out, sems) = refs[: 2 * count], refs[2 * count :]
    crossed, swapped = arrays[: count + 1], arrays[count + 1 :] + arrays[count : count + 1]
    group = lax.axis_index("groups")
    slot = hot_slot(popular, plan.homed, mirror_of(plan, lax.axis_index("replica")))
    for adapter in range(count):
        for g in range(2):

            @pl.when((slot == adapter) & (group == g))
            def _():
                copies = []
                for j in range(plan.half):
                    row, col = plan.place(j)
                    part, row = divmod(row, plan.cut)
                    src = (crossed if part == g else swapped)[adapter]
                    copies.append(
                        pltpu.make_async_copy(
                            src.at[pl.ds(row, ROWS), pl.ds(col, plan.spread)],
                            out.at[pl.ds(j * ROWS, ROWS)],
                            sems.at[j],
                        )
                    )
                    copies[-1].start()
                for copy in copies:
                    copy.wait()


def relay_kernel(plan, got, reply, far, out, held, meta, sems):
    copies = [
        pltpu.make_async_copy(got.at[:, pl.ds(plan.meta_at, LANES)], meta, sems.at[0]),
        pltpu.make_async_copy(
            got.at[:, pl.ds(plan.tok_cols, plan.spread)],
            held,
            sems.at[1],
        ),
        pltpu.make_async_copy(reply, out.at[:, pl.ds(0, plan.back_cols)], sems.at[2]),
    ]
    for copy in copies:
        copy.start()
    for copy in copies[:2]:
        copy.wait()
    wanted = meta[...].astype(F32).astype(jnp.int32)[:, plan.sections : plan.sections + 1]
    shape = (plan.packed, plan.packed)
    inner = lax.broadcasted_iota(jnp.int32, shape, 0) % ROWS
    index = lax.broadcasted_iota(jnp.int32, shape, 1)
    near = as_hot(index == wanted * ROWS + inner)
    away = as_hot(index + plan.packed == wanted * ROWS + inner)
    total = jnp.dot(near, held[...], preferred_element_type=F32)
    total += jnp.dot(away, far[...], preferred_element_type=F32)
    out[:, plan.back_cols :] = total.astype(BF16)
    copies[2].wait()


def near_final_kernel(plan, ids1, ids2, counts, back, base1, base2, out1, out2, down, up):
    for j in range(plan.half):
        row, first = plan.place(j)
        rows = slice(row, row + ROWS)
        for at in range(0, plan.spread, LANES):
            col = first + at
            start = plan.back_cols + at
            tile = back[j * ROWS : (j + 1) * ROWS, start : start + LANES]
            if col < plan.width:
                down[0, rows, col : col + LANES] = tile
            else:
                up[0, rows, col - plan.width : col - plan.width + LANES] = tile
    index = lax.broadcasted_iota(jnp.int32, (plan.tok, plan.packed), 1)
    inner = index % ROWS
    for b, (ids, base, out) in enumerate(((ids1, base1, out1), (ids2, base2, out2))):
        _, _, peer, pos = route((ids[...] // plan.homed) % plan.half, 1)
        cell = pos + b * plan.per
        own = index // ROWS == peer
        total = base[...]
        for s in range(plan.sections):
            if (b + 1) * plan.per <= s * ROWS or b * plan.per >= (s + 1) * ROWS:
                continue
            hot = as_hot(own & (inner + s * ROWS == cell))
            at = s * plan.feature
            total += jnp.dot(hot, back[:, at : at + plan.feature], preferred_element_type=F32)
        valid = lax.broadcasted_iota(jnp.int32, total.shape, 0) < counts[b, 0]
        out[...] = jnp.where(valid, total, 0.0).astype(BF16)


def call(kernel, name, out_shape, operands, in_specs, out_specs, scratch=(), cost=0, mib=63):
    return pl.pallas_call(
        kernel,
        out_shape=out_shape,
        in_specs=in_specs,
        out_specs=out_specs,
        scratch_shapes=list(scratch),
        compiler_params=pltpu.CompilerParams(vmem_limit_bytes=mib * 1024 * 1024),
        cost_estimate=pl.CostEstimate(flops=0, bytes_accessed=cost, transcendentals=0)
        if cost
        else None,
        name=name,
    )(*operands)


def exchange(x, n, **kwargs):
    x = x.reshape(n, x.shape[0] // n, x.shape[1])
    x = lax.all_to_all(x, "replica", split_axis=0, concat_axis=0, tiled=True, **kwargs)
    return x.reshape(n * x.shape[1], x.shape[2])


def local(
    first_activations,
    second_activations,
    first_adapter_ids,
    second_adapter_ids,
    valid_row_counts,
    popular_adapters,
    replica_hosting,
    value_weight_base,
    adapter_down_factors,
    adapter_up_factors,
):
    tok, width = first_activations.shape
    homed, _, rank = adapter_down_factors.shape
    feature = adapter_up_factors.shape[2]
    plan = Plan(lax.axis_size("replica"), tok, width, rank, feature, homed)
    wide = Wide(plan, lax.axis_size("groups"))
    down = jnp.swapaxes(adapter_down_factors, 1, 2)
    up = adapter_up_factors
    ids1 = first_adapter_ids.reshape(1, tok)
    ids2 = second_adapter_ids.reshape(1, tok)
    anywhere = pl.BlockSpec(memory_space=pl.ANY)
    vmem = pl.BlockSpec(memory_space=pltpu.VMEM)
    smem = pl.BlockSpec(memory_space=pltpu.SMEM)
    dma = pltpu.SemaphoreType.DMA
    sources = (
        ids1,
        ids2,
        popular_adapters,
        replica_hosting,
        first_activations,
        second_activations,
        down,
        up,
    )
    first_scratch = [
        pltpu.VMEM((2, 1, tok), jnp.int32),
        pltpu.SMEM(popular_adapters.shape, jnp.int32),
        pltpu.SMEM(replica_hosting.shape, jnp.int32),
        pltpu.VMEM((2 * tok, width), BF16),
    ]
    base1 = jnp.dot(first_activations, value_weight_base, preferred_element_type=F32)
    base2 = jnp.dot(second_activations, value_weight_base, preferred_element_type=F32)
    down_joined, up_joined = down.reshape(homed * rank, width), up.reshape(homed * rank, feature)

    def shape(*dims):
        return jax.ShapeDtypeStruct(dims, BF16)

    if wide.fits:
        half = wide.half
        count = homed + 1
        halves = [list(range(half)), list(range(half, wide.peers))]
        across = [(0, 1), (1, 0)]
        mirror = [(i, i ^ half) for i in range(wide.peers)]
        cuts = call(
            functools.partial(cut_kernel, wide),
            "cut",
            [shape(wide.cut, wide.factor)] * count,
            (down, up),
            [anywhere] * 2,
            [vmem] * count,
            [dma((2 * count,))],
        )
        crossed = [lax.ppermute(c, "replica", mirror) for c in cuts]
        swapped = [lax.ppermute(c, "groups", across) for c in crossed[: homed - 1]]
        sent = call(
            functools.partial(near_pack_kernel, wide),
            "pack",
            shape(wide.packed, wide.cols),
            sources,
            [anywhere] * 8,
            anywhere,
            first_scratch
            + [
                pltpu.VMEM((wide.packed, wide.cols), BF16),
                dma((12,)),
                dma((4 * wide.sections + 1,)),
                dma((2 * half,)),
            ],
            cost=4 * wide.packed * wide.cols,
        )
        got = exchange(sent, half, axis_index_groups=halves)
        got, *arrived = lax.optimization_barrier((got, *crossed))
        hot = call(
            functools.partial(far_hot_kernel, wide),
            "far_hot",
            shape(wide.packed, wide.spread),
            (popular_adapters, *arrived, *swapped),
            [smem] + [anywhere] * (2 * homed),
            vmem,
            [dma((half,))],
        )
        far = exchange(hot, half, axis_index_groups=halves)
        rows = 2 * homed * rank
        reply = call(
            functools.partial(near_home_kernel, wide),
            "home",
            shape(wide.packed, wide.back_cols),
            (got, down_joined, up_joined, *crossed, *swapped),
            [anywhere] * (3 + 2 * homed),
            vmem,
            [
                pltpu.VMEM((wide.sections * wide.packed, width), BF16),
                pltpu.VMEM((wide.packed, LANES), BF16),
                pltpu.VMEM((rows, width), BF16),
                pltpu.VMEM((rows, feature), BF16),
                dma((2 + 2 * homed + 4 * (wide.sections + 1 + 2 * homed),)),
            ],
        )
        answer = call(
            functools.partial(relay_kernel, wide),
            "relay",
            shape(wide.packed, wide.ret_cols),
            (got, reply, far),
            [anywhere, anywhere, vmem],
            vmem,
            [
                pltpu.VMEM((wide.packed, wide.spread), BF16),
                pltpu.VMEM((wide.packed, LANES), BF16),
                dma((3,)),
            ],
            mib=24,
        )
        back = exchange(answer, half, axis_index_groups=halves)
        finish = functools.partial(near_final_kernel, wide)
    else:
        sent = call(
            functools.partial(pack_kernel, plan),
            "pack",
            shape(plan.packed, plan.cols),
            sources,
            [anywhere] * 8,
            anywhere,
            first_scratch
            + [
                pltpu.VMEM((rank, width + feature), BF16),
                pltpu.VMEM((plan.packed, plan.cols), BF16),
                dma((14,)),
                dma((4 * plan.full + 2 * plan.rest + 1,)),
            ],
        )
        got = exchange(sent, plan.peers)
        reply = call(
            functools.partial(home_kernel, plan),
            "home",
            shape(plan.packed, plan.ret_cols),
            (down_joined, up_joined, got),
            [vmem, vmem, anywhere],
            anywhere,
            [
                pltpu.VMEM((plan.packed, plan.cols), BF16),
                pltpu.VMEM((plan.packed, plan.ret_cols), BF16),
                dma((1 + 2 * plan.full + plan.rest,)),
                dma((2,)),
            ],
        )
        back = exchange(reply, plan.peers)
        finish = functools.partial(final_kernel, plan)
    out1, out2, resident_down, resident_up = call(
        finish,
        "finish",
        [shape(tok, feature), shape(tok, feature), shape(1, rank, width), shape(1, rank, feature)],
        (ids1, ids2, valid_row_counts, back, base1, base2),
        [vmem, vmem, smem, vmem, vmem, vmem],
        [vmem] * 4,
        mib=24,
    )
    return out1, out2, jnp.swapaxes(resident_down, 1, 2), resident_up


def solution(mesh):
    return jax.shard_map(
        local,
        mesh=mesh,
        in_specs=(
            P(("groups", "replica"), None),
            P(("groups", "replica"), None),
            P(("groups", "replica")),
            P(("groups", "replica")),
            P(None, ("groups", "replica")),
            P("groups"),
            P(("groups", "replica")),
            P(),
            P("replica", None, None),
            P("replica", None, None),
        ),
        out_specs=(
            P(("groups", "replica"), None),
            P(("groups", "replica"), None),
            P(("groups", "replica"), None, None),
            P(("groups", "replica"), None, None),
        ),
        check_vma=False,
    )
```

```python
import functools

import jax
import jax.numpy as jnp
from jax import lax
from jax.experimental import pallas as pl
from jax.experimental.pallas import tpu as pltpu
from jax.sharding import PartitionSpec as P

LANES = 128
ROWS = 16
CHUNK = 256
F32 = jnp.float32
BF16 = jnp.bfloat16
NT = (((1,), (1,)), ((), ()))


class Plan:
    def __init__(self, peers, tok, width, rank, feature, homed):
        self.peers, self.tok, self.width, self.rank = peers, tok, width, rank
        self.feature, self.homed = feature, homed
        self.cap = max(2, 3 * tok // (2 * peers))
        combined = 2 * self.cap
        self.full = combined // ROWS
        left = combined - self.full * ROWS
        if left > 8:
            self.full, left = self.full + 1, 0
        self.rest = left > 0
        self.sections = self.full + self.rest
        self.packed = peers * ROWS
        self.joined = homed * rank
        self.tok_cols = self.full * width + self.rest * (width // 2)
        self.back_cols = self.full * feature + self.rest * (feature // 2)
        self.col_tiles = (width + feature) // LANES
        tiles = (rank // ROWS) * self.col_tiles
        share = -(-tiles // peers)
        while self.col_tiles % share:
            share += 1
        self.per_group = self.col_tiles // share
        self.holders = tiles // share
        self.spread = share * LANES
        self.meta_at = self.tok_cols + self.spread
        self.cols = self.meta_at + LANES
        self.ret_cols = self.spread + self.back_cols

    def row_chunks(self, count):
        size = min(CHUNK, count * ROWS)
        return [(i, size) for i in range(0, count * ROWS, size)]


def route(ids, homed):
    n = ids.shape[1]
    ids = jnp.broadcast_to(ids, (n, n))
    peer_row = ids // homed
    peer_col = jnp.transpose(ids.astype(F32)).astype(jnp.int32) // homed
    same = peer_row == peer_col
    above = lax.broadcasted_iota(jnp.int32, (n, n), 0)
    along = lax.broadcasted_iota(jnp.int32, (n, n), 1)
    pos_row = jnp.sum(jnp.where(same & (above < along), 1, 0), axis=0, keepdims=True)
    pos_col = jnp.sum(jnp.where(same & (along < above), 1, 0), axis=1, keepdims=True)
    return peer_row[0:1, :], pos_row, peer_col[:, 0:1], pos_col


def as_hot(mask):
    return jnp.where(mask, 1.0, 0.0).astype(BF16)


def pack_kernel(plan, ids1, ids2, popular, hosting, x1, x2, down, up, out, *scratch):
    ids, hot_ids, host_id, x, hot, packed, sems, out_sems = scratch
    me = lax.axis_index("replica")
    count = plan.peers
    quarter = plan.width // 4
    loads = [
        pltpu.make_async_copy(popular, hot_ids, sems.at[0]),
        pltpu.make_async_copy(hosting, host_id, sems.at[1]),
        pltpu.make_async_copy(ids1, ids.at[0], sems.at[2]),
        pltpu.make_async_copy(ids2, ids.at[1], sems.at[3]),
    ]
    for c in range(4):
        cols = pl.ds(c * quarter, quarter)
        for b, src in enumerate((x1, x2)):
            loads.append(
                pltpu.make_async_copy(
                    src.at[:, cols],
                    x.at[pl.ds(b * plan.tok, plan.tok), cols],
                    sems.at[4 + 2 * c + b],
                )
            )
    for load in loads:
        load.start()
    loads[0].wait()
    loads[1].wait()
    slot = jnp.int32(0)
    for i in range(hot_ids.shape[0]):
        adapter = hot_ids[i]
        slot = jnp.where(adapter // plan.homed == me, adapter % plan.homed, slot)
    wanted = hot_ids[host_id[0]] // plan.homed
    hots = [
        pltpu.make_async_copy(down.at[slot], hot.at[:, pl.ds(0, plan.width)], sems.at[12]),
        pltpu.make_async_copy(up.at[slot], hot.at[:, pl.ds(plan.width, plan.feature)], sems.at[13]),
    ]
    for load in hots:
        load.start()
    loads[2].wait()
    loads[3].wait()
    peers, cells, slots = [], [], []
    for b in range(2):
        peer, pos, _, _ = route(ids[b], plan.homed)
        peers.append(peer)
        cells.append(pos + b * plan.cap)
        slots.append((ids[b] % plan.homed).astype(F32))
    peer, cell = jnp.concatenate(peers, axis=1), jnp.concatenate(cells, axis=1)
    slots = jnp.concatenate(slots, axis=1)
    chunks = plan.row_chunks(count)
    stores = []

    def send(at, size):
        cols = pl.ds(at, size)
        stores.append(
            pltpu.make_async_copy(packed.at[:, cols], out.at[:, cols], out_sems.at[len(stores)])
        )
        stores[-1].start()

    masks = []
    for start, size in chunks:
        index = lax.broadcasted_iota(jnp.int32, (size, 2 * plan.tok), 0) + start
        own = index // ROWS == peer
        inner = index % ROWS
        sets = [own & (inner + s * ROWS == cell) for s in range(plan.full)]
        marks = list(sets)
        if plan.rest:
            low = own & (inner + plan.full * ROWS == cell) & (inner < 8)
            high = own & (inner - 8 + plan.full * ROWS == cell) & (inner >= 8)
            sets += [low, high]
            marks.append(low | high)
        masks.append([as_hot(m) for m in sets])
        lane = lax.broadcasted_iota(jnp.int32, (size, LANES), 1)
        meta = jnp.where(lane == plan.sections, wanted.astype(F32), 0.0)
        for s, mark in enumerate(marks):
            value = jnp.sum(jnp.where(mark, slots, 0.0), axis=1, keepdims=True)
            meta = jnp.where(lane == s, value, meta)
        packed[start : start + size, plan.meta_at :] = meta.astype(BF16)

    for c in range(4):
        loads[4 + 2 * c].wait()
        loads[5 + 2 * c].wait()
        cols = slice(c * quarter, (c + 1) * quarter)
        for (start, size), hot_masks in zip(chunks, masks):
            for s in range(plan.full):
                value = jnp.dot(hot_masks[s], x[:, cols], preferred_element_type=F32)
                at = s * plan.width + c * quarter
                packed[start : start + size, at : at + quarter] = value.astype(BF16)
        for s in range(plan.full):
            send(s * plan.width + c * quarter, quarter)
    if plan.rest:
        at = plan.full * plan.width
        for c in range(2):
            for (start, size), hot_masks in zip(chunks, masks):
                both = jnp.concatenate(hot_masks[plan.full :], axis=1)
                source = jnp.concatenate(
                    [
                        x[:, c * quarter : (c + 1) * quarter],
                        x[:, (c + 2) * quarter : (c + 3) * quarter],
                    ],
                    axis=0,
                )
                value = jnp.dot(both, source, preferred_element_type=F32)
                packed[start : start + size, at + c * quarter : at + (c + 1) * quarter] = (
                    value.astype(BF16)
                )
            send(at + c * quarter, quarter)
    for load in hots:
        load.wait()
    for i in range(count):
        group, col = divmod(i % plan.holders, plan.per_group)
        col *= plan.spread
        packed[i * ROWS : (i + 1) * ROWS, plan.tok_cols : plan.meta_at] = hot[
            group * ROWS : (group + 1) * ROWS, col : col + plan.spread
        ]
    send(plan.tok_cols, plan.spread + LANES)
    for store in stores:
        store.wait()


def home_kernel(plan, down, up, source, out, got, reply, sems, out_sems):
    bounds = [(plan.tok_cols, plan.spread + LANES)]
    bounds += [(c, plan.width // 2) for c in range(0, plan.tok_cols, plan.width // 2)]
    loads = []
    for at, size in bounds:
        cols = pl.ds(at, size)
        loads.append(
            pltpu.make_async_copy(source.at[:, cols], got.at[:, cols], sems.at[len(loads)])
        )
        loads[-1].start()

    def ready(i):
        loads[i].wait()

    chunks = plan.row_chunks(plan.peers)
    ready(0)
    metas = []
    for start, n in chunks:
        rows = slice(start, start + n)
        meta = got[rows, plan.meta_at :].astype(F32).astype(jnp.int32)
        metas.append(meta)
        wide = lax.broadcasted_iota(jnp.int32, (n, plan.packed), 1)
        inner = lax.broadcasted_iota(jnp.int32, (n, plan.packed), 0) % ROWS
        pick = as_hot(wide == meta[:, plan.sections : plan.sections + 1] * ROWS + inner)
        reply[rows, : plan.spread] = jnp.dot(
            pick, got[:, plan.tok_cols : plan.meta_at], preferred_element_type=F32
        ).astype(BF16)
    relayed = pltpu.make_async_copy(
        reply.at[:, pl.ds(0, plan.spread)], out.at[:, pl.ds(0, plan.spread)], out_sems.at[0]
    )
    relayed.start()
    half = plan.width // 2
    group = plan.joined
    for s in range(plan.sections):
        at = s * plan.width
        split = s == plan.full
        ready(1 + 2 * s)
        for i, ((start, n), meta) in enumerate(zip(chunks, metas)):
            rows = slice(start, start + n)
            low = lax.dot_general(
                got[rows, at : at + half], down[:, :half], NT, preferred_element_type=F32
            )
            if not split:
                if i == 0:
                    ready(2 + 2 * s)
                low += lax.dot_general(
                    got[rows, at + half : at + plan.width],
                    down[:, half:],
                    NT,
                    preferred_element_type=F32,
                )
                slot = meta[:, s : s + 1]
            else:
                high = lax.dot_general(
                    got[rows, at : at + half], down[:, half:], NT, preferred_element_type=F32
                )
                low = low.reshape(n // ROWS, 2, 8, group)[:, 0]
                high = high.reshape(n // ROWS, 2, 8, group)[:, 1]
                low = (low + high).reshape(n // 2, group)
                slot = meta.reshape(n // ROWS, 2, 8, LANES)[:, 0].reshape(n // 2, LANES)
                slot = slot[:, s : s + 1]
            column = lax.broadcasted_iota(jnp.int32, low.shape, 1) // plan.rank
            kept = jnp.where(column == slot, low, 0.0).astype(BF16)
            delta = jnp.dot(kept, up[...], preferred_element_type=F32)
            to = plan.spread + s * plan.feature
            if split:
                delta = delta.reshape(n // ROWS, 8, plan.feature)
                middle = plan.feature // 2
                delta = jnp.concatenate([delta[..., :middle], delta[..., middle:]], axis=1)
                delta = delta.reshape(n, middle)
            reply[rows, to : to + delta.shape[1]] = delta.astype(BF16)
    answered = pltpu.make_async_copy(
        reply.at[:, pl.ds(plan.spread, plan.back_cols)],
        out.at[:, pl.ds(plan.spread, plan.back_cols)],
        out_sems.at[1],
    )
    answered.start()
    relayed.wait()
    answered.wait()


def final_kernel(plan, ids1, ids2, counts, back, base1, base2, out1, out2, down, up):
    for d in range(plan.holders):
        rows = slice((d // plan.per_group) * ROWS, (d // plan.per_group + 1) * ROWS)
        for j in range(0, plan.spread, LANES):
            col = (d % plan.per_group) * plan.spread + j
            tile = back[d * ROWS : (d + 1) * ROWS, j : j + LANES]
            if col < plan.width:
                down[0, rows, col : col + LANES] = tile
            else:
                up[0, rows, col - plan.width : col - plan.width + LANES] = tile
    index = lax.broadcasted_iota(jnp.int32, (plan.tok, plan.packed), 1)
    inner = index % ROWS
    middle = plan.feature // 2
    for b, (ids, base, out) in enumerate(((ids1, base1, out1), (ids2, base2, out2))):
        _, _, peer, pos = route(ids[...], plan.homed)
        cell = pos + b * plan.cap
        own = index // ROWS == peer
        total = base[...]
        for s in range(plan.full):
            if (b + 1) * plan.cap <= s * ROWS or b * plan.cap >= (s + 1) * ROWS:
                continue
            hot = as_hot(own & (inner + s * ROWS == cell))
            at = plan.spread + s * plan.feature
            total += jnp.dot(hot, back[:, at : at + plan.feature], preferred_element_type=F32)
        if plan.rest and (b + 1) * plan.cap > plan.full * ROWS:
            at = plan.spread + plan.full * plan.feature
            values = back[:, at : at + middle]
            low = as_hot(own & (inner + plan.full * ROWS == cell) & (inner < 8))
            high = as_hot(own & (inner - 8 + plan.full * ROWS == cell) & (inner >= 8))
            total += jnp.concatenate(
                [jnp.dot(hot, values, preferred_element_type=F32) for hot in (low, high)], axis=1
            )
        valid = lax.broadcasted_iota(jnp.int32, total.shape, 0) < counts[b, 0]
        out[...] = jnp.where(valid, total, 0.0).astype(BF16)


class Wide:
    def __init__(self, plan, groups):
        self.peers, self.tok, self.width, self.rank = plan.peers, plan.tok, plan.width, plan.rank
        self.feature, self.homed, self.groups = plan.feature, plan.homed, groups
        self.half = self.peers // 2
        self.per = 2 * plan.cap
        self.sections = -(-2 * self.per // ROWS)
        self.packed = self.half * ROWS
        self.tok_cols = self.sections * self.width
        self.factor = self.width + self.feature
        col_tiles = self.factor // LANES
        tiles = (self.rank // ROWS) * col_tiles
        self.share = tiles // max(self.half, 1)
        self.spread = self.share * LANES
        self.meta_at = self.tok_cols + self.spread
        self.cols = self.meta_at + LANES
        self.back_cols = self.sections * self.feature
        self.ret_cols = self.back_cols + self.spread
        self.per_group = col_tiles // max(self.share, 1)
        self.cut = self.rank // 2
        self.fits = (
            groups == 2
            and self.half > 0
            and self.peers & (self.peers - 1) == 0
            and self.peers <= 16
            and tiles % self.half == 0
            and self.share > 0
            and col_tiles % self.share == 0
            and self.cut % ROWS == 0
        )

    def chunks(self, group):
        return [(a, group) for a in range(self.homed)] + [(self.homed - 1, 1 - group)]

    def place(self, j):
        group, col = divmod(j, self.per_group)
        return group * ROWS, col * self.spread


def cut_kernel(plan, down, up, *refs):
    outs, sems = refs[:-1], refs[-1]
    copies = []
    for (adapter, part), out in zip(plan.chunks(lax.axis_index("groups")), outs):
        rows = pl.ds(pl.multiple_of(part * plan.cut, ROWS), plan.cut)
        for src, cols in (
            (down, pl.ds(0, plan.width)),
            (up, pl.ds(plan.width, plan.feature)),
        ):
            copies.append(
                pltpu.make_async_copy(
                    src.at[adapter, rows], out.at[:, cols], sems.at[len(copies)]
                )
            )
    for copy in copies:
        copy.start()
    for copy in copies:
        copy.wait()


def mirror_of(plan, me):
    return me + plan.half - 2 * plan.half * (me // plan.half)


def hot_slot(popular, homed, home):
    slot = jnp.int32(0)
    for i in range(popular.shape[0]):
        adapter = popular[i]
        slot = jnp.where(adapter // homed == home, adapter % homed, slot)
    return slot


def near_pack_kernel(plan, ids1, ids2, popular, hosting, x1, x2, down, up, out, *scratch):
    ids, hot_ids, host_id, x, packed, sems, out_sems, hot_sems = scratch
    me = lax.axis_index("replica")
    side = me // plan.half
    quarter = plan.width // 4
    loads = [
        pltpu.make_async_copy(popular, hot_ids, sems.at[0]),
        pltpu.make_async_copy(hosting, host_id, sems.at[1]),
        pltpu.make_async_copy(ids1, ids.at[0], sems.at[2]),
        pltpu.make_async_copy(ids2, ids.at[1], sems.at[3]),
    ]
    for c in range(4):
        cols = pl.ds(c * quarter, quarter)
        for b, src in enumerate((x1, x2)):
            loads.append(
                pltpu.make_async_copy(
                    src.at[:, cols],
                    x.at[pl.ds(b * plan.tok, plan.tok), cols],
                    sems.at[4 + 2 * c + b],
                )
            )
    for load in loads:
        load.start()
    for load in loads[:4]:
        load.wait()
    slot = hot_slot(hot_ids, plan.homed, me)
    hots = []
    for j in range(plan.half):
        row, col = plan.place(j)
        rows, to = pl.ds(row, ROWS), pl.ds(j * ROWS, ROWS)
        inside = min(plan.spread, max(plan.width - col, 0))
        if inside:
            hots.append((down.at[slot, rows, pl.ds(col, inside)], to, 0, inside))
        if inside < plan.spread:
            from_up = pl.ds(col + inside - plan.width, plan.spread - inside)
            hots.append((up.at[slot, rows, from_up], to, inside, plan.spread - inside))
    stores = []
    for i, (src, to, at, size) in enumerate(hots):
        hots[i] = pltpu.make_async_copy(
            src, packed.at[to, pl.ds(plan.tok_cols + at, size)], hot_sems.at[i]
        )
        hots[i].start()
    wanted = hot_ids[host_id[0]] // plan.homed
    wanted = wanted % plan.half + jnp.where(wanted // plan.half == side, 0, plan.half)
    peers, cells, slots = [], [], []
    for b in range(2):
        home = ids[b] // plan.homed
        peer, pos, _, _ = route(home % plan.half, 1)
        peers.append(peer)
        cells.append(pos + b * plan.per)
        far = jnp.where(home // plan.half == side, 0, plan.homed)
        slots.append((ids[b] % plan.homed + far).astype(F32))
    peer, cell = jnp.concatenate(peers, axis=1), jnp.concatenate(cells, axis=1)
    slots = jnp.concatenate(slots, axis=1)
    index = lax.broadcasted_iota(jnp.int32, (plan.packed, 2 * plan.tok), 0)
    own = index // ROWS == peer
    inner = index % ROWS
    masks = []
    for s in range(plan.sections):
        masks.append(own & (inner + s * ROWS == cell))
    mask = jnp.concatenate([as_hot(m) for m in masks], axis=0)

    def send(at, size):
        stores.append(
            pltpu.make_async_copy(
                packed.at[:, pl.ds(at, size)],
                out.at[:, pl.ds(at, size)],
                out_sems.at[len(stores)],
            )
        )
        stores[-1].start()

    for c in range(4):
        loads[4 + 2 * c].wait()
        loads[5 + 2 * c].wait()
        value = jnp.dot(
            mask, x[:, c * quarter : (c + 1) * quarter], preferred_element_type=F32
        ).astype(BF16)
        for s in range(plan.sections):
            at = s * plan.width + c * quarter
            packed[:, at : at + quarter] = value[s * plan.packed : (s + 1) * plan.packed]
            send(at, quarter)
        if c == 2:
            lane = lax.broadcasted_iota(jnp.int32, (plan.packed, LANES), 1)
            meta = jnp.where(lane == plan.sections, wanted.astype(F32), 0.0)
            for s, mark in enumerate(masks):
                column = jnp.sum(jnp.where(mark, slots, 0.0), axis=1, keepdims=True)
                meta = jnp.where(lane == s, column, meta)
            packed[:, plan.meta_at :] = meta.astype(BF16)
            for load in hots:
                load.wait()
            send(plan.tok_cols, plan.spread + LANES)
    for store in stores:
        store.wait()


def near_home_kernel(plan, got, down, up, *refs):
    count = plan.homed
    arrays, out = refs[: 2 * count], refs[2 * count]
    x, meta, weights, ups, reply, sems = refs[2 * count + 1 :]
    group = lax.axis_index("groups")
    pieces, joined = 4, plan.homed * plan.rank
    size = plan.width // pieces
    used = []

    def load(src, dst):
        used.append(pltpu.make_async_copy(src, dst, sems.at[len(used)]))
        used[-1].start()
        return used[-1]

    first = [load(got.at[:, pl.ds(plan.meta_at, LANES)], meta)]
    far = []
    halves = plan.chunks(group) + plan.chunks(1 - group)[: count - 1]
    for (adapter, part), array in zip(halves, arrays):
        at = joined + adapter * plan.rank + part * plan.cut
        far.append((array, pl.ds(pl.multiple_of(at, ROWS), plan.cut)))
    steps = []
    for c in range(pieces):
        cols = pl.ds(c * size, size)
        step = []
        for s in range(plan.sections):
            step.append(
                load(
                    got.at[:, pl.ds(s * plan.width + c * size, size)],
                    x.at[pl.ds(s * plan.packed, plan.packed), cols],
                )
            )
        step.append(load(down.at[:, cols], weights.at[pl.ds(0, joined), cols]))
        for array, rows in far:
            step.append(load(array.at[:, cols], weights.at[rows, cols]))
        steps.append(step)
    first.append(load(up, ups.at[pl.ds(0, joined)]))
    for array, rows in far:
        first.append(load(array.at[:, pl.ds(plan.width, plan.feature)], ups.at[rows]))
    total = None
    for c, step in enumerate(steps):
        for copy in step:
            copy.wait()
        cols = slice(c * size, (c + 1) * size)
        term = lax.dot_general(x[:, cols], weights[:, cols], NT, preferred_element_type=F32)
        total = term if total is None else total + term
    for copy in first:
        copy.wait()
    slots = meta[...].astype(F32).astype(jnp.int32)
    slots = jnp.concatenate([slots[:, s : s + 1] for s in range(plan.sections)], axis=0)
    column = lax.broadcasted_iota(jnp.int32, total.shape, 1) // plan.rank
    kept = jnp.where(column == slots, total, 0.0).astype(BF16)
    delta = jnp.dot(kept, ups[...], preferred_element_type=F32).astype(BF16)
    for s in range(plan.sections):
        reply[:, s * plan.feature : (s + 1) * plan.feature] = delta[
            s * plan.packed : (s + 1) * plan.packed
        ]
    load(reply, out.at[:, pl.ds(0, plan.back_cols)]).wait()


def far_hot_kernel(plan, popular, *refs):
    count = plan.homed
    arrays, (out, sems) = refs[: 2 * count], refs[2 * count :]
    crossed, swapped = arrays[: count + 1], arrays[count + 1 :] + arrays[count : count + 1]
    group = lax.axis_index("groups")
    slot = hot_slot(popular, plan.homed, mirror_of(plan, lax.axis_index("replica")))
    for adapter in range(count):
        for g in range(2):

            @pl.when((slot == adapter) & (group == g))
            def _():
                copies = []
                for j in range(plan.half):
                    row, col = plan.place(j)
                    part, row = divmod(row, plan.cut)
                    src = (crossed if part == g else swapped)[adapter]
                    copies.append(
                        pltpu.make_async_copy(
                            src.at[pl.ds(row, ROWS), pl.ds(col, plan.spread)],
                            out.at[pl.ds(j * ROWS, ROWS)],
                            sems.at[j],
                        )
                    )
                    copies[-1].start()
                for copy in copies:
                    copy.wait()


def relay_kernel(plan, got, reply, far, out, held, meta, sent, sems):
    copies = [
        pltpu.make_async_copy(got.at[:, pl.ds(plan.meta_at, LANES)], meta, sems.at[0]),
        pltpu.make_async_copy(
            got.at[:, pl.ds(plan.tok_cols, plan.spread)],
            held,
            sems.at[1],
        ),
    ]
    for copy in copies:
        copy.start()
    for copy in copies:
        copy.wait()
    wanted = meta[...].astype(F32).astype(jnp.int32)[:, plan.sections : plan.sections + 1]
    shape = (plan.packed, plan.packed)
    inner = lax.broadcasted_iota(jnp.int32, shape, 0) % ROWS
    index = lax.broadcasted_iota(jnp.int32, shape, 1)
    near = as_hot(index == wanted * ROWS + inner)
    away = as_hot(index + plan.packed == wanted * ROWS + inner)
    total = jnp.dot(near, held[...], preferred_element_type=F32)
    total += jnp.dot(away, far[...], preferred_element_type=F32)
    sent[...] = total.astype(BF16)
    last = pltpu.make_async_copy(sent, out.at[:, pl.ds(plan.back_cols, plan.spread)], sems.at[2])
    last.start()
    last.wait()


def near_final_kernel(plan, ids1, ids2, counts, back, base1, base2, out1, out2, down, up):
    for j in range(plan.half):
        row, first = plan.place(j)
        rows = slice(row, row + ROWS)
        for at in range(0, plan.spread, LANES):
            col = first + at
            start = plan.back_cols + at
            tile = back[j * ROWS : (j + 1) * ROWS, start : start + LANES]
            if col < plan.width:
                down[0, rows, col : col + LANES] = tile
            else:
                up[0, rows, col - plan.width : col - plan.width + LANES] = tile
    index = lax.broadcasted_iota(jnp.int32, (plan.tok, plan.packed), 1)
    inner = index % ROWS
    for b, (ids, base, out) in enumerate(((ids1, base1, out1), (ids2, base2, out2))):
        _, _, peer, pos = route((ids[...] // plan.homed) % plan.half, 1)
        cell = pos + b * plan.per
        own = index // ROWS == peer
        total = base[...]
        for s in range(plan.sections):
            if (b + 1) * plan.per <= s * ROWS or b * plan.per >= (s + 1) * ROWS:
                continue
            hot = as_hot(own & (inner + s * ROWS == cell))
            at = s * plan.feature
            total += jnp.dot(hot, back[:, at : at + plan.feature], preferred_element_type=F32)
        valid = lax.broadcasted_iota(jnp.int32, total.shape, 0) < counts[b, 0]
        out[...] = jnp.where(valid, total, 0.0).astype(BF16)


def call(kernel, name, out_shape, operands, in_specs, out_specs, scratch=(), cost=0, mib=63, aliases=None):
    return pl.pallas_call(
        kernel,
        out_shape=out_shape,
        in_specs=in_specs,
        out_specs=out_specs,
        scratch_shapes=list(scratch),
        input_output_aliases=aliases or {},
        compiler_params=pltpu.CompilerParams(vmem_limit_bytes=mib * 1024 * 1024),
        cost_estimate=pl.CostEstimate(flops=0, bytes_accessed=cost, transcendentals=0)
        if cost
        else None,
        name=name,
    )(*operands)


def exchange(x, n, **kwargs):
    x = x.reshape(n, x.shape[0] // n, x.shape[1])
    x = lax.all_to_all(x, "replica", split_axis=0, concat_axis=0, tiled=True, **kwargs)
    return x.reshape(n * x.shape[1], x.shape[2])


def local(
    first_activations,
    second_activations,
    first_adapter_ids,
    second_adapter_ids,
    valid_row_counts,
    popular_adapters,
    replica_hosting,
    value_weight_base,
    adapter_down_factors,
    adapter_up_factors,
):
    tok, width = first_activations.shape
    homed, _, rank = adapter_down_factors.shape
    feature = adapter_up_factors.shape[2]
    plan = Plan(lax.axis_size("replica"), tok, width, rank, feature, homed)
    wide = Wide(plan, lax.axis_size("groups"))
    down = jnp.swapaxes(adapter_down_factors, 1, 2)
    up = adapter_up_factors
    ids1 = first_adapter_ids.reshape(1, tok)
    ids2 = second_adapter_ids.reshape(1, tok)
    anywhere = pl.BlockSpec(memory_space=pl.ANY)
    vmem = pl.BlockSpec(memory_space=pltpu.VMEM)
    smem = pl.BlockSpec(memory_space=pltpu.SMEM)
    dma = pltpu.SemaphoreType.DMA
    sources = (
        ids1,
        ids2,
        popular_adapters,
        replica_hosting,
        first_activations,
        second_activations,
        down,
        up,
    )
    first_scratch = [
        pltpu.VMEM((2, 1, tok), jnp.int32),
        pltpu.SMEM(popular_adapters.shape, jnp.int32),
        pltpu.SMEM(replica_hosting.shape, jnp.int32),
        pltpu.VMEM((2 * tok, width), BF16),
    ]
    base1 = jnp.dot(first_activations, value_weight_base, preferred_element_type=F32)
    base2 = jnp.dot(second_activations, value_weight_base, preferred_element_type=F32)
    down_joined, up_joined = down.reshape(homed * rank, width), up.reshape(homed * rank, feature)

    def shape(*dims):
        return jax.ShapeDtypeStruct(dims, BF16)

    if wide.fits:
        half = wide.half
        count = homed + 1
        halves = [list(range(half)), list(range(half, wide.peers))]
        across = [(0, 1), (1, 0)]
        mirror = [(i, i ^ half) for i in range(wide.peers)]
        cuts = call(
            functools.partial(cut_kernel, wide),
            "cut",
            [shape(wide.cut, wide.factor)] * count,
            (down, up),
            [anywhere] * 2,
            [vmem] * count,
            [dma((2 * count,))],
        )
        crossed = [lax.ppermute(c, "replica", mirror) for c in cuts]
        swapped = [lax.ppermute(c, "groups", across) for c in crossed[: homed - 1]]
        sent = call(
            functools.partial(near_pack_kernel, wide),
            "pack",
            shape(wide.packed, wide.cols),
            sources,
            [anywhere] * 8,
            anywhere,
            first_scratch
            + [
                pltpu.VMEM((wide.packed, wide.cols), BF16),
                dma((12,)),
                dma((4 * wide.sections + 1,)),
                dma((2 * half,)),
            ],
            cost=4 * wide.packed * wide.cols,
        )
        got = exchange(sent, half, axis_index_groups=halves)
        got, *arrived = lax.optimization_barrier((got, *crossed))
        hot = call(
            functools.partial(far_hot_kernel, wide),
            "far_hot",
            shape(wide.packed, wide.spread),
            (popular_adapters, *arrived, *swapped),
            [smem] + [anywhere] * (2 * homed),
            vmem,
            [dma((half,))],
            mib=16,
        )
        far = exchange(hot, half, axis_index_groups=halves)
        rows = 2 * homed * rank
        reply = call(
            functools.partial(near_home_kernel, wide),
            "home",
            shape(wide.packed, wide.ret_cols),
            (got, down_joined, up_joined, *crossed, *swapped),
            [anywhere] * (3 + 2 * homed),
            anywhere,
            [
                pltpu.VMEM((wide.sections * wide.packed, width), BF16),
                pltpu.VMEM((wide.packed, LANES), BF16),
                pltpu.VMEM((rows, width), BF16),
                pltpu.VMEM((rows, feature), BF16),
                pltpu.VMEM((wide.packed, wide.back_cols), BF16),
                dma((3 + 2 * homed + 4 * (wide.sections + 1 + 2 * homed),)),
            ],
        )
        answer = call(
            functools.partial(relay_kernel, wide),
            "relay",
            shape(wide.packed, wide.ret_cols),
            (got, reply, far),
            [anywhere, anywhere, vmem],
            anywhere,
            [
                pltpu.VMEM((wide.packed, wide.spread), BF16),
                pltpu.VMEM((wide.packed, LANES), BF16),
                pltpu.VMEM((wide.packed, wide.spread), BF16),
                dma((3,)),
            ],
            mib=24,
            aliases={1: 0},
        )
        back = exchange(answer, half, axis_index_groups=halves)
        finish = functools.partial(near_final_kernel, wide)
    else:
        sent = call(
            functools.partial(pack_kernel, plan),
            "pack",
            shape(plan.packed, plan.cols),
            sources,
            [anywhere] * 8,
            anywhere,
            first_scratch
            + [
                pltpu.VMEM((rank, width + feature), BF16),
                pltpu.VMEM((plan.packed, plan.cols), BF16),
                dma((14,)),
                dma((4 * plan.full + 2 * plan.rest + 1,)),
            ],
        )
        got = exchange(sent, plan.peers)
        reply = call(
            functools.partial(home_kernel, plan),
            "home",
            shape(plan.packed, plan.ret_cols),
            (down_joined, up_joined, got),
            [vmem, vmem, anywhere],
            anywhere,
            [
                pltpu.VMEM((plan.packed, plan.cols), BF16),
                pltpu.VMEM((plan.packed, plan.ret_cols), BF16),
                dma((1 + 2 * plan.full + plan.rest,)),
                dma((2,)),
            ],
        )
        back = exchange(reply, plan.peers)
        finish = functools.partial(final_kernel, plan)
    out1, out2, resident_down, resident_up = call(
        finish,
        "finish",
        [shape(tok, feature), shape(tok, feature), shape(1, rank, width), shape(1, rank, feature)],
        (ids1, ids2, valid_row_counts, back, base1, base2),
        [vmem, vmem, smem, vmem, vmem, vmem],
        [vmem] * 4,
        mib=24,
    )
    return out1, out2, jnp.swapaxes(resident_down, 1, 2), resident_up


def solution(mesh):
    return jax.shard_map(
        local,
        mesh=mesh,
        in_specs=(
            P(("groups", "replica"), None),
            P(("groups", "replica"), None),
            P(("groups", "replica")),
            P(("groups", "replica")),
            P(None, ("groups", "replica")),
            P("groups"),
            P(("groups", "replica")),
            P(),
            P("replica", None, None),
            P("replica", None, None),
        ),
        out_specs=(
            P(("groups", "replica"), None),
            P(("groups", "replica"), None),
            P(("groups", "replica"), None, None),
            P(("groups", "replica"), None, None),
        ),
        check_vma=False,
    )
```
